512 devices in a mesh: section: 16 (over y, core), tp: 32 (over z, x).
Axes of the slice: x: 4, y: 8, z: 8, core: 2. Of those that a mesh axis runs over, the one named last changes fastest.
Arguments:
- hidden: bfloat16 [16, 2, 256, 8192], P('section', None, None, 'tp'), may hold values from -400 to 400
- gain: float32 [16, 8192], P('section', 'tp'), may hold values from 0.5 to 1.5
- key_grad: bfloat16 [16, 2, 256, 1024], P('section', None, 'tp'), may hold values from -24 to 24
- master: float32 [16, 8192, 1024], P('section', 'tp'), may hold values from -0.0625 to 0.0625
- moment: float32 [16, 8192, 1024], P('section', 'tp'), may hold values from -0.00048828125 to 0.00048828125
- second: float32 [16, 8192, 1024], P('section', 'tp'), may hold values from 2.2351742e-11 to 2.23517418e-10
- overflow: int32 [16], P('section'), may hold values from 0 to 2
Outputs:
- grad_input: bfloat16 [16, 2, 256, 8192], P('section', None, None, 'tp')
- step: float32 [16, 8192, 1024], P('section', 'tp')
The draws below stay inside these ranges and needn't reach their ends.
All inputs are finite; a program needn't handle non-finite values.
Results may differ from the reference program's by a relative error of at most 0.0049.
Values may be sent and summed in bfloat16 or wider, within the bound.
No kernel may reach another device: no remote copies, remote signals or barrier semaphores. Data moves between devices by JAX's collectives and lax.ppermute only.
A program may use at most 64 MiB of HBM per device.

```python
import math
import jax
import jax.numpy as jnp
from jax import lax

D = 8192
MB = 2
SEQ = 256
KVW = 1024
SECTIONS = 16
ALLP = 134217728


def draw_hidden(key, part):
    key = jax.random.fold_in(key, 11)
    key_base, key_rows, key_cols = jax.random.split(key, 3)
    shape = (SECTIONS, MB, SEQ, D)
    base = jnp.clip(jax.random.normal(key_base, shape, jnp.float32), -4.0, 4.0)
    row_scale = jnp.exp(jax.random.uniform(key_rows, (SECTIONS, MB, SEQ, 1), jnp.float32, 0.0, math.log(10.0)))
    col_scale = jnp.exp(jax.random.uniform(key_cols, (1, 1, 1, D), jnp.float32, 0.0, math.log(3.3)))
    trend = jnp.power(3.0, jnp.arange(D, dtype=jnp.float32) / max(D - 1, 1))
    return (base * row_scale * col_scale * trend).astype(jnp.bfloat16)


def draw_key_grad(key, part):
    key = jax.random.fold_in(key, 23)
    key_base = jax.random.fold_in(key, 0)
    shape = (SECTIONS, MB, SEQ, KVW)
    base = jnp.clip(jax.random.normal(key_base, shape, jnp.float32), -4.0, 4.0)
    layer_scale = 2.0 * jnp.power(3.0, jnp.arange(SECTIONS, dtype=jnp.float32) / max(SECTIONS - 1, 1))
    return (base * layer_scale[:, None, None, None]).astype(jnp.bfloat16)


def draw_second(key, part):
    key = jax.random.fold_in(key, 37)
    shape = (SECTIONS, D, KVW)
    values = jnp.exp(jax.random.uniform(key, shape, jnp.float32, math.log(0.003), math.log(0.03)))
    return values / ALLP


def set_ends(array, stream_key, low, top_value):
    index_at = [jax.random.randint(jax.random.fold_in(stream_key, axis), (), 0, length) for axis, length in enumerate(array.shape)]
    main_axis = array.shape.index(max(array.shape))
    neighbour = index_at[:main_axis] + [(index_at[main_axis] + 1) % array.shape[main_axis]] + index_at[main_axis + 1:]
    return array.at[tuple(index_at)].set(low).at[tuple(neighbour)].set(top_value)


def steps_of(rng, dims, pieces, least, top_value):
    loudness, own = 1.0, jax.random.fold_in(rng, 6)
    for axis_at, parts in pieces:
        draws = jnp.exp(jax.random.uniform(jax.random.fold_in(own, axis_at), (parts,), jnp.float32, least / len(pieces), top_value / len(pieces)))
        loudness = loudness * jnp.repeat(draws, dims[axis_at] // parts).reshape([-1 if axis == axis_at else 1 for axis in range(len(dims))])
    return loudness


def normal_values(stream_key, shape, width, reach, cuts=(), kind=jnp.bfloat16):
    factor_of = steps_of(stream_key, shape, cuts, -0.22, 0.18) if cuts else 1.0
    entries = jax.random.normal(stream_key, shape, jnp.float32) * width * factor_of
    return jnp.minimum(jnp.maximum(entries, -reach), reach).astype(kind)


def setup_inputs(seed: int = 0) -> dict:
    streams_of = jax.random.split(jax.random.key(seed), 8)
    hidden = draw_hidden(jax.random.fold_in(streams_of[7], 71), 0)
    gain = jnp.clip(1.0 + 0.1 * jax.random.normal(streams_of[1], (SECTIONS, D), jnp.float32), 0.5, 1.5)
    key_grad = draw_key_grad(jax.random.fold_in(streams_of[7], 71), 0)
    master = normal_values(streams_of[3], (SECTIONS, D, KVW), D ** -0.5, 0.0625, ((0, 16), (1, 32)), jnp.float32)
    moment = normal_values(streams_of[4], (SECTIONS, D, KVW), ALLP ** -0.5, 0.00048828125, ((0, 16), (1, 32)), jnp.float32)
    second = draw_second(jax.random.fold_in(streams_of[7], 71), 0)
    overflow = set_ends(jax.random.randint(streams_of[6], (SECTIONS,), 0, 3), jax.random.fold_in(streams_of[6], 1), 0, 2).astype(jnp.int32)
    return {"hidden": hidden, "gain": gain, "key_grad": key_grad, "master": master, "moment": moment, "second": second, "overflow": overflow}


beta_one = 0.9
beta_two = 0.999
decay = 0.1
clip_norm = 1.0
step_count = 10

def section_terms(hidden, gain, key_grad, master):
    values = hidden.astype(jnp.float32)
    inv_rms = lax.rsqrt(lax.optimization_barrier(jnp.mean(values * values, axis=-1)) + 1e-05)
    normed = values * inv_rms[..., None]
    inputs = (gain * normed).astype(jnp.bfloat16)
    weight = master.astype(jnp.bfloat16)
    flat_in = inputs.reshape(-1, D)
    flat_key = key_grad.reshape(-1, KVW)
    grad_w = jnp.dot(flat_in.T, flat_key, preferred_element_type=jnp.float32)
    grad_h = jnp.dot(flat_key, weight.T, preferred_element_type=jnp.float32).reshape(MB, SEQ, D)
    gated = gain * grad_h
    row_mean = lax.optimization_barrier(jnp.mean(gated * normed, axis=-1))
    branch = inv_rms[..., None] * (gated - normed * row_mean[..., None])
    return (branch, grad_w)

def reference(hidden, gain, key_grad, master, moment, second, overflow):

    def visit(running, items):
        layer_in, layer_gain, layer_key, layer_master = items
        branch, grad_w = section_terms(layer_in, layer_gain, layer_key, layer_master)
        running = running + branch
        return (running, (running.astype(jnp.bfloat16), grad_w))
    start_sum = jnp.zeros((MB, SEQ, D), jnp.float32)
    _, outputs = lax.scan(visit, start_sum, (hidden, gain, key_grad, master), reverse=True)
    grad_input, grad_all = outputs
    factor = jnp.where(overflow == 0, 1.0, jnp.where(overflow == 1, 0.5, 0.0)).astype(jnp.float32)
    gradient = factor[:, None, None] * grad_all
    grad_norm = jnp.sqrt(jnp.sum(gradient * gradient))
    clip_factor = jnp.minimum(1.0, clip_norm / (grad_norm + 1e-06))
    clipped = clip_factor * gradient
    moment_new = beta_one * moment + (1.0 - beta_one) * clipped
    second_new = beta_two * second + (1.0 - beta_two) * clipped * clipped
    bias_one = 1.0 - beta_one ** step_count
    bias_two = 1.0 - beta_two ** step_count
    update = moment_new / bias_one / (jnp.sqrt(second_new / bias_two) + 1e-08) + decay * master
    keep_mask = jnp.where(overflow == 2, 0.0, 1.0).astype(jnp.float32)
    step = keep_mask[:, None, None] * update
    return (grad_input, step)
```

```python
import jax
import jax.numpy as jnp
from jax import lax
from jax.sharding import PartitionSpec as P

D = 8192
TP = 32
SEC = 16

beta_one = 0.9
beta_two = 0.999
decay = 0.1
clip_norm = 1.0
step_count = 10


def swap(blocks, axis):
    return lax.all_to_all(blocks, axis, split_axis=0, concat_axis=0, tiled=True)


def gather(value, axis, size):
    return swap(jnp.broadcast_to(value[None], (size,) + value.shape), axis)


def on_device(hidden, gain, key_grad, master, moment, second, overflow):
    f32, bf16 = jnp.float32, jnp.bfloat16
    x = hidden[0].reshape(512, 256).T.astype(f32)
    rows = gather(key_grad[0], "tp", TP)
    rows = rows.transpose(1, 0, 2, 3).reshape(512, 1024)
    sums = jnp.sum(x * x, axis=0).reshape(4, 128)
    total_sq = jnp.sum(gather(sums, "tp", TP), axis=0).reshape(1, 512)
    inv = lax.rsqrt(total_sq / D + 1e-05)
    col = gain[0][:, None]
    gx = x * col
    weight = master[0].astype(bf16)
    grad_h = lax.dot_general(weight, rows, (((1,), (1,)), ((), ())), preferred_element_type=f32)
    grad_w = jnp.dot((gx * inv).astype(bf16), rows, preferred_element_type=f32)
    flag = overflow[0]
    factor = jnp.where(flag == 0, 1.0, jnp.where(flag == 1, 0.5, 0.0)).astype(f32)
    gradient = factor * grad_w
    own_sq = jnp.sum(gradient * gradient)
    inner = jnp.sum(gx * grad_h, axis=0).reshape(4, 128)
    packed = jnp.concatenate([inner, jnp.full((4, 128), own_sq, f32)], axis=0)
    packed = jnp.sum(gather(packed, "tp", TP), axis=0)
    row_mean = packed[:4].reshape(1, 512) * inv / D
    branch = inv * (col * grad_h - x * inv * row_mean)
    layer_sq = packed[4:5, 0:1]
    branch = branch.astype(bf16).reshape(SEC, 16, 512)
    hi = layer_sq.astype(bf16)
    lo = (layer_sq - hi.astype(f32)).astype(bf16)
    extra = jnp.concatenate([jnp.broadcast_to(hi, (4, 512)), jnp.broadcast_to(lo, (4, 512))], axis=0)
    send = jnp.concatenate([branch, jnp.broadcast_to(extra[None], (SEC, 8, 512))], axis=1)
    got = swap(send, "section")
    norm_sq = jnp.sum(got[:, 16, 0].astype(f32) + got[:, 20, 0].astype(f32))
    running = jnp.zeros((16, 512), f32)
    outs = [None] * SEC
    for s in range(SEC - 1, -1, -1):
        running = running + got[s, :16].astype(f32)
        outs[s] = running.astype(bf16)
    back = swap(jnp.stack(outs), "section")
    grad_input = back.reshape(256, 512).T.reshape(1, 2, 256, 256)
    clip_factor = jnp.minimum(1.0, clip_norm / (jnp.sqrt(norm_sq) + 1e-06))
    clipped = clip_factor * gradient
    moment_new = beta_one * moment[0] + (1.0 - beta_one) * clipped
    second_new = beta_two * second[0] + (1.0 - beta_two) * clipped * clipped
    bias_one = 1.0 - beta_one**step_count
    bias_two = 1.0 - beta_two**step_count
    update = moment_new / bias_one / (jnp.sqrt(second_new / bias_two) + 1e-08) + decay * master[0]
    keep_mask = jnp.where(flag == 2, 0.0, 1.0).astype(f32)
    step = (keep_mask * update)[None]
    return (grad_input, step)


def solution(mesh):
    return jax.shard_map(
        on_device,
        mesh=mesh,
        in_specs=(
            P("section", None, None, "tp"),
            P("section", "tp"),
            P("section", None, "tp", None),
            P("section", "tp", None),
            P("section", "tp", None),
            P("section", "tp", None),
            P("section"),
        ),
        out_specs=(P("section", None, None, "tp"), P("section", "tp", None)),
        check_vma=False,
    )
```

```python
import functools

import jax
import jax.numpy as jnp
from jax import lax
from jax.experimental import pallas as pl
from jax.experimental.pallas import tpu as pltpu
from jax.sharding import PartitionSpec as P

D = 8192
SEC = 16
NZ, NX = 8, 4
TP = NZ * NX
TOK = 512
F = 256
K = 1024
f32, bf16 = jnp.float32, jnp.bfloat16

beta_one = 0.9
beta_two = 0.999
decay = 0.1
clip_norm = 1.0
step_count = 10

VM = pl.BlockSpec(memory_space=pltpu.VMEM)
SM = pl.BlockSpec(memory_space=pltpu.SMEM)


def call(body, out_shape, in_specs, out_specs, flops=0, data=0, scratch=()):
    return pl.pallas_call(
        body,
        out_shape=out_shape,
        in_specs=in_specs,
        out_specs=out_specs,
        scratch_shapes=list(scratch),
        compiler_params=pltpu.CompilerParams(vmem_limit_bytes=32 * 1024 * 1024),
        cost_estimate=pl.CostEstimate(flops=flops, bytes_accessed=data, transcendentals=0),
    )


def shift_z(value, k):
    pairs = [(z * NX + x, (z + k) % NZ * NX + x) for z in range(NZ) for x in range(NX)]
    return lax.ppermute(value, "tp", pairs)


def shift_x(value, k):
    pairs = [(z * NX + x, z * NX + (x + k) % NX) for z in range(NZ) for x in range(NX)]
    return lax.ppermute(value, "tp", pairs)


def sum_tp(value):
    parts = [shift_z(value, k) for k in range(1, NZ)]
    value = sum(parts, value)
    parts = [shift_x(value, k) for k in range(1, NX)]
    return [value] + parts


def turn_kernel(x_ref, xt_ref, sums_ref):
    x = x_ref[...].astype(f32).reshape(2, TP, 8, F)
    x = jnp.concatenate([x[0][:, None], x[1][:, None]], axis=1).reshape(TOK, F)
    xt = x.T
    xt_ref[...] = xt
    sums_ref[...] = jnp.sum(xt * xt, axis=0, keepdims=True)


def main_kernel(
    place_ref, factor_ref, x_ref, s0, s1, s2, s3, gain_ref, master_ref, r0, r1, r2, r3,
    gh_ref, gw_ref, inv_ref, packed_ref, rows_ref, gx_ref,
):
    z, x = place_ref[0], place_ref[1]
    for kx, block in enumerate((r0, r1, r2, r3)):
        for kz in range(NZ):
            slot = ((z + NZ - kz) % NZ) * NX + (x + NX - kx) % NX
            rows_ref[pl.ds(pl.multiple_of(slot * 16, 16), 16), :] = block[kz]
    total = s0[...] + s1[...] + s2[...] + s3[...]
    inv = lax.rsqrt(total * (1.0 / D) + 1e-05)
    inv_ref[...] = inv
    col = gain_ref[...]
    gx = x_ref[...] * col
    weight = master_ref[...].astype(bf16)
    gx_ref[...] = (gx * inv).astype(bf16)
    for n in range(2):
        cols = slice(n * 256, (n + 1) * 256)
        gh = lax.dot_general(
            weight, rows_ref[cols, :], (((1,), (1,)), ((), ())), preferred_element_type=f32
        )
        gh_ref[:, cols] = gh
        packed_ref[:, cols] = jnp.sum(gx[:, cols] * gh, axis=0, keepdims=True)
    factor = factor_ref[0]
    square = jnp.zeros((1, 256), f32)
    for n in range(4):
        cols = slice(n * 256, (n + 1) * 256)
        part = factor * jnp.dot(gx_ref[...], rows_ref[:, cols], preferred_element_type=f32)
        gw_ref[:, cols] = part
        square = square + jnp.sum(part * part, axis=0, keepdims=True)
    packed_ref[:, TOK:] = jnp.broadcast_to(jnp.sum(square, axis=1, keepdims=True), (1, 128))


def branch_kernel(x_ref, gh_ref, inv_ref, gain_ref, p0, p1, p2, p3, send_ref):
    packed = p0[...] + p1[...] + p2[...] + p3[...]
    inv = inv_ref[...]
    row_mean = packed[:, :TOK] * (inv * (1.0 / D))
    branch = inv * (gain_ref[...] * gh_ref[...] - x_ref[...] * (inv * row_mean))
    send_ref[:, 0:16, :] = branch.astype(bf16).reshape(SEC, 16, TOK)
    layer_sq = jnp.broadcast_to(packed[:, TOK : TOK + 1], (16, TOK))
    hi = layer_sq.astype(bf16)
    lo = (layer_sq - hi.astype(f32)).astype(bf16)
    low_rows = lax.broadcasted_iota(jnp.int32, (16, TOK), 0) >= 8
    both = jnp.where(low_rows, lo.astype(f32), hi.astype(f32)).astype(bf16)
    send_ref[:, 16:32, :] = jnp.broadcast_to(both[None], (SEC, 16, TOK))


def suffix_kernel(got_ref, back_ref, clip_ref):
    running = jnp.zeros((16, TOK), f32)
    norm = jnp.zeros((16, TOK), f32)
    for s in range(SEC - 1, -1, -1):
        running = running + got_ref[s, 0:16, :].astype(f32)
        back_ref[s] = running.astype(bf16)
        norm = norm + got_ref[s, 16:32, :].astype(f32)
    norm_sq = norm[0:1, 0:128] + norm[8:9, 0:128]
    clip_ref[...] = jnp.minimum(1.0, clip_norm / (jnp.sqrt(norm_sq) + 1e-06))


def unturn_kernel(back_ref, out_ref):
    out = back_ref[...].reshape(F, TOK).astype(f32).T
    out = out.reshape(TP, 2, 8, F)
    for m in range(2):
        out_ref[m] = out[:, m].reshape(256, F).astype(bf16)


def swap(blocks, axis):
    return lax.all_to_all(blocks, axis, split_axis=0, concat_axis=0, tiled=True)


def sds(shape, dtype=f32):
    return jax.ShapeDtypeStruct(shape, dtype)


def on_device(hidden, gain, key_grad, master, moment, second, overflow):
    at = lax.axis_index("tp")
    place = jnp.stack([at // NX, at % NX]).astype(jnp.int32)
    flag = overflow[0]
    factor = jnp.where(flag == 0, 1.0, jnp.where(flag == 1, 0.5, 0.0)).astype(f32)
    col = gain.reshape(F, 1)

    xt, sums = call(
        turn_kernel, (sds((F, TOK)), sds((1, TOK))), [VM], (VM, VM), 3 * F * TOK, 3 * F * TOK * 2
    )(hidden[0])
    sums = sum_tp(sums)
    own = key_grad.reshape(16, K)
    blocks = jnp.stack([own] + [shift_z(own, k) for k in range(1, NZ)])
    blocks = [blocks] + [shift_x(blocks, k) for k in range(1, NX)]

    gh, gw, inv, packed = call(
        main_kernel,
        (sds((F, TOK)), sds((F, K)), sds((1, TOK)), sds((1, TOK + 128))),
        [SM, SM] + [VM] * 11,
        (VM,) * 4,
        4 * F * TOK * K,
        6 * 1024 * 1024,
        [pltpu.VMEM((TOK, K), bf16), pltpu.VMEM((F, TOK), bf16)],
    )(place, factor[None], xt, *sums, col, master[0], *blocks)
    packed = sum_tp(packed)
    send = call(
        branch_kernel, sds((SEC, 32, TOK), bf16), [VM] * 8, VM, 6 * F * TOK, 2 * 1024 * 1024
    )(xt, gh, inv, col, *packed)
    got = swap(send, "section")
    back, clip = call(
        suffix_kernel, (sds((SEC, 16, TOK), bf16), sds((1, 128))), [VM], (VM, VM), 4 * F * TOK, 1024 * 1024
    )(got)
    back = swap(back, "section")
    grad_input = call(unturn_kernel, sds((2, 256, F), bf16), [VM], VM, F * TOK, 1024 * 1024)(back)

    clipped = clip[0, 0] * gw
    moment_new = beta_one * moment[0] + (1.0 - beta_one) * clipped
    second_new = beta_two * second[0] + (1.0 - beta_two) * clipped * clipped
    bias_one = 1.0 - beta_one**step_count
    bias_two = 1.0 - beta_two**step_count
    update = moment_new / bias_one / (jnp.sqrt(second_new / bias_two) + 1e-08) + decay * master[0]
    keep_mask = jnp.where(flag == 2, 0.0, 1.0).astype(f32)
    step = (keep_mask * update)[None]
    return (grad_input[None], step)


def solution(mesh):
    return jax.shard_map(
        on_device,
        mesh=mesh,
        in_specs=(
            P("section", None, None, "tp"),
            P("section", "tp"),
            P("section", None, "tp", None),
            P("section", "tp", None),
            P("section", "tp", None),
            P("section", "tp", None),
            P("section"),
        ),
        out_specs=(P("section", None, None, "tp"), P("section", "tp", None)),
        check_vma=False,
    )
```

```python
import jax
import jax.numpy as jnp
from jax import lax
from jax.experimental import pallas as pl
from jax.experimental.pallas import tpu as pltpu
from jax.sharding import Mesh, PartitionSpec as P

D = 8192
NY, NC, NZ, NX = 8, 2, 8, 4
TP = NZ * NX
TOK = 512
F = 256
K = 1024
f32, bf16 = jnp.float32, jnp.bfloat16

beta_one = 0.9
beta_two = 0.999
decay = 0.1
clip_norm = 1.0
step_count = 10

VM = pl.BlockSpec(memory_space=pltpu.VMEM)
SM = pl.BlockSpec(memory_space=pltpu.SMEM)


def call(body, out_shape, n_in, flops=0, data=0, scratch=(), scalars=0):
    outs = (VM,) * len(out_shape) if isinstance(out_shape, tuple) else VM
    return pl.pallas_call(
        body,
        out_shape=out_shape,
        in_specs=[SM] * scalars + [VM] * n_in,
        out_specs=outs,
        scratch_shapes=list(scratch),
        compiler_params=pltpu.CompilerParams(vmem_limit_bytes=32 * 1024 * 1024),
        cost_estimate=pl.CostEstimate(flops=flops, bytes_accessed=data, transcendentals=0),
    )


def sds(shape, dtype=f32):
    return jax.ShapeDtypeStruct(shape, dtype)


def swap(blocks, axis):
    return lax.all_to_all(blocks, axis, split_axis=0, concat_axis=0, tiled=True)


def split_rows(row):
    rows = jnp.concatenate([row[:, i * 128 : (i + 1) * 128] for i in range(4)], axis=0)
    high = rows.astype(bf16).astype(f32)
    low = rows - high
    return jnp.concatenate([high, low, jnp.zeros((8, 128), f32)], axis=0).astype(bf16)


def join_rows(rows):
    rows = rows.astype(f32)
    return rows[0:4] + rows[4:8]


def as_row(rows):
    return jnp.concatenate([rows[i : i + 1] for i in range(4)], axis=1)


def first_kernel(x_ref, key_ref, xt_ref, send_ref):
    x = x_ref[...].astype(f32).reshape(2, TP, 8, F)
    x = jnp.concatenate([x[0][:, None], x[1][:, None]], axis=1).reshape(TOK, F)
    xt = x.T
    xt_ref[...] = xt
    sums = split_rows(jnp.sum(xt * xt, axis=0, keepdims=True))
    for peer in range(NZ):
        for c in range(8):
            send_ref[peer, c * 16 : (c + 1) * 16, :] = key_ref[:, c * 128 : (c + 1) * 128]
        send_ref[peer, 128:144, :] = sums


def middle_kernel(got_ref, send_ref):
    total = jnp.zeros((4, 128), f32)
    for z in range(NZ):
        total = total + join_rows(got_ref[z, 128:144, :])
    sums = split_rows(as_row(total))
    for peer in range(NX):
        for z in range(NZ):
            send_ref[peer, z * 128 : (z + 1) * 128, :] = got_ref[z, 0:128, :]
        send_ref[peer, 1024:1040, :] = sums


def main_kernel(
    factor_ref, x_ref, got_ref, gain_ref, master_ref, gh_ref, gw_ref, inv_ref, send_ref, rows_ref, gx_ref
):
    for x in range(NX):
        for z in range(NZ):
            slot = z * NX + x
            for c in range(8):
                rows_ref[slot * 16 : (slot + 1) * 16, c * 128 : (c + 1) * 128] = got_ref[
                    x, z * 128 + c * 16 : z * 128 + (c + 1) * 16, :
                ]
    total = jnp.zeros((4, 128), f32)
    for x in range(NX):
        total = total + join_rows(got_ref[x, 1024:1040, :])
    inv = lax.rsqrt(as_row(total) * (1.0 / D) + 1e-05)
    inv_ref[...] = inv
    gx = x_ref[...] * gain_ref[...]
    weight = master_ref[...].astype(bf16)
    gx_ref[...] = (gx * inv).astype(bf16)
    for n in range(2):
        cols = slice(n * 256, (n + 1) * 256)
        gh = lax.dot_general(
            weight, rows_ref[cols, :], (((1,), (1,)), ((), ())), preferred_element_type=f32
        )
        gh_ref[:, cols] = gh
        inner = jnp.sum(gx[:, cols] * gh, axis=0, keepdims=True)
        for peer in range(NZ):
            send_ref[peer, 2 * n : 2 * n + 1, :] = inner[:, 0:128]
            send_ref[peer, 2 * n + 1 : 2 * n + 2, :] = inner[:, 128:256]
    factor = factor_ref[0]
    square = jnp.zeros((1, 256), f32)
    for n in range(4):
        cols = slice(n * 256, (n + 1) * 256)
        part = factor * jnp.dot(gx_ref[...], rows_ref[:, cols], preferred_element_type=f32)
        gw_ref[:, cols] = part
        square = square + jnp.sum(part * part, axis=0, keepdims=True)
    own_sq = jnp.broadcast_to(jnp.sum(square, axis=1, keepdims=True), (4, 128))
    for peer in range(NZ):
        send_ref[peer, 4:8, :] = own_sq


def sum_kernel(got_ref, send_ref):
    total = got_ref[0]
    for z in range(1, NZ):
        total = total + got_ref[z]
    for peer in range(NX):
        send_ref[peer] = total


def branch_kernel(x_ref, gh_ref, inv_ref, gain_ref, got_ref, branch_ref, send_ref):
    packed = got_ref[0] + got_ref[1] + got_ref[2] + got_ref[3]
    inv = inv_ref[...]
    row_mean = as_row(packed[0:4]) * (inv * (1.0 / D))
    branch = inv * (gain_ref[...] * gh_ref[...] - x_ref[...] * (inv * row_mean))
    branch_ref[...] = branch
    sent = branch.astype(bf16)
    layer_sq = split_rows(jnp.concatenate([packed[4:5]] * 4, axis=1))
    for j in range(NY):
        for q in range(4):
            send_ref[j, q * 32 : (q + 1) * 32, :] = sent[j * 32 : (j + 1) * 32, q * 128 : (q + 1) * 128]
        send_ref[j, 128:144, :] = layer_sq


def suffix_kernel(got_ref, back_ref, norm_ref):
    running = jnp.zeros((128, 128), f32)
    norm = jnp.zeros((4, 128), f32)
    for y in range(NY - 1, -1, -1):
        back_ref[y] = running.astype(bf16)
        running = running + got_ref[y, 0:128, :].astype(f32)
        norm = norm + join_rows(got_ref[y, 128:144, :])
    norm_ref[...] = jnp.concatenate([norm, norm], axis=0)


def pair_kernel(core_ref, back_ref, branch_ref, own_ref, send_ref):
    upper = core_ref[0] == 1
    for j in range(NY):
        for q in range(4):
            rows, cols = slice(j * 32, (j + 1) * 32), slice(q * 128, (q + 1) * 128)
            later = back_ref[j, q * 32 : (q + 1) * 32, :].astype(f32)
            whole = later + branch_ref[rows, cols]
            own_ref[rows, cols] = whole
            send_ref[rows, cols] = jnp.where(upper, whole, later)


def last_kernel(own_ref, other_ref, out_ref):
    out = (own_ref[...] + other_ref[...]).T.reshape(TP, 2, 8, F)
    for m in range(2):
        out_ref[m] = out[:, m].reshape(256, F).astype(bf16)


def on_device(hidden, gain, key_grad, master, moment, second, overflow):
    flag = overflow[0]
    factor = jnp.where(flag == 0, 1.0, jnp.where(flag == 1, 0.5, 0.0)).astype(f32)
    col = gain.reshape(F, 1)
    core = lax.axis_index("core").astype(jnp.int32)[None]

    xt, send = call(first_kernel, (sds((F, TOK)), sds((NZ, 144, 128), bf16)), 2, 3 * F * TOK, 3 * F * TOK * 2)(
        hidden[0], key_grad.reshape(16, K)
    )
    got = swap(send, "z")
    send = call(middle_kernel, sds((NX, 1040, 128), bf16), 1, 0, 2 * 1024 * 1024)(got)
    got = swap(send, "x")
    gh, gw, inv, send = call(
        main_kernel,
        (sds((F, TOK)), sds((F, K)), sds((1, TOK)), sds((NZ, 8, 128))),
        4,
        4 * F * TOK * K,
        6 * 1024 * 1024,
        [pltpu.VMEM((TOK, K), bf16), pltpu.VMEM((F, TOK), bf16)],
        1,
    )(factor[None], xt, got, col, master[0])
    got = swap(send, "z")
    send = call(sum_kernel, sds((NX, 8, 128)), 1)(got)
    got = swap(send, "x")
    branch, send = call(
        branch_kernel, (sds((F, TOK)), sds((NY, 144, 128), bf16)), 5, 6 * F * TOK, 2 * 1024 * 1024
    )(xt, gh, inv, col, got)
    got = swap(send, "y")
    back, norm = call(
        suffix_kernel, (sds((NY, 128, 128), bf16), sds((8, 128))), 1, 4 * F * TOK, 1024 * 1024
    )(got)
    back = swap(back, "y")
    norm_other = lax.ppermute(norm, "core", [(0, 1), (1, 0)])
    own, send = call(pair_kernel, (sds((F, TOK)), sds((F, TOK))), 2, F * TOK, 2 * 1024 * 1024, (), 1)(
        core, back, branch
    )
    other = lax.ppermute(send, "core", [(0, 1), (1, 0)])
    grad_input = call(last_kernel, sds((2, 256, F), bf16), 2, F * TOK, 1024 * 1024)(own, other)

    grad_norm = jnp.sqrt(norm[0, 0] + norm_other[0, 0])
    clip_factor = jnp.minimum(1.0, clip_norm / (grad_norm + 1e-06))
    clipped = clip_factor * gw
    moment_new = beta_one * moment[0] + (1.0 - beta_one) * clipped
    second_new = beta_two * second[0] + (1.0 - beta_two) * clipped * clipped
    bias_one = 1.0 - beta_one**step_count
    bias_two = 1.0 - beta_two**step_count
    update = moment_new / bias_one / (jnp.sqrt(second_new / bias_two) + 1e-08) + decay * master[0]
    keep_mask = jnp.where(flag == 2, 0.0, 1.0).astype(f32)
    step = (keep_mask * update)[None]
    return (grad_input[None], step)


def solution(mesh):
    fine = Mesh(mesh.devices.reshape(NY, NC, NZ, NX), ("y", "core", "z", "x"))
    sec, tp = ("y", "core"), ("z", "x")
    return jax.shard_map(
        on_device,
        mesh=fine,
        in_specs=(
            P(sec, None, None, tp),
            P(sec, tp),
            P(sec, None, tp, None),
            P(sec, tp, None),
            P(sec, tp, None),
            P(sec, tp, None),
            P(sec),
        ),
        out_specs=(P(sec, None, None, tp), P(sec, tp, None)),
        check_vma=False,
    )
```

```python
import jax
import jax.numpy as jnp
from jax import lax
from jax.experimental import pallas as pl
from jax.experimental.pallas import tpu as pltpu
from jax.sharding import PartitionSpec as P

D = 8192
SEC, TP = 16, 32
TOK = 512
F = 256
K = 1024
f32, bf16 = jnp.float32, jnp.bfloat16

beta_one = 0.9
beta_two = 0.999
decay = 0.1
clip_norm = 1.0
step_count = 10

VM = pl.BlockSpec(memory_space=pltpu.VMEM)
SM = pl.BlockSpec(memory_space=pltpu.SMEM)


def call(body, out_shape, n_in, flops=0, data=0, scratch=(), scalars=0):
    outs = (VM,) * len(out_shape) if isinstance(out_shape, tuple) else VM
    return pl.pallas_call(
        body,
        out_shape=out_shape,
        in_specs=[SM] * scalars + [VM] * n_in,
        out_specs=outs,
        scratch_shapes=list(scratch),
        compiler_params=pltpu.CompilerParams(vmem_limit_bytes=32 * 1024 * 1024),
        cost_estimate=pl.CostEstimate(flops=flops, bytes_accessed=data, transcendentals=0),
    )


def sds(shape, dtype=f32):
    return jax.ShapeDtypeStruct(shape, dtype)


def swap(blocks, axis):
    return lax.all_to_all(blocks, axis, split_axis=0, concat_axis=0, tiled=True)


def split_rows(row):
    rows = jnp.concatenate([row[:, i * 128 : (i + 1) * 128] for i in range(4)], axis=0)
    high = rows.astype(bf16).astype(f32)
    low = rows - high
    return jnp.concatenate([high, low, jnp.zeros((8, 128), f32)], axis=0).astype(bf16)


def join_rows(rows):
    rows = rows.astype(f32)
    return rows[0:4] + rows[4:8]


def as_row(rows):
    return jnp.concatenate([rows[i : i + 1] for i in range(4)], axis=1)


def first_kernel(x_hbm, key_hbm, xt_ref, send_ref, x_ref, key_ref, sems):
    x_copy = pltpu.make_async_copy(x_hbm, x_ref, sems.at[0])
    key_copy = pltpu.make_async_copy(key_hbm, key_ref, sems.at[1])
    x_copy.start()
    key_copy.start()
    key_copy.wait()
    for peer in range(TP):
        for c in range(8):
            send_ref[peer, c * 16 : (c + 1) * 16, :] = key_ref[:, c * 128 : (c + 1) * 128]
    x_copy.wait()
    x = x_ref[...].astype(f32).reshape(2, TP, 8, F)
    x = jnp.concatenate([x[0][:, None], x[1][:, None]], axis=1).reshape(TOK, F)
    xt = x.T
    xt_ref[...] = xt
    sums = split_rows(jnp.sum(xt * xt, axis=0, keepdims=True))
    for peer in range(TP):
        send_ref[peer, 128:144, :] = sums


def weight_kernel(master_ref, gain_ref, pin_ref, weight_ref, col_ref):
    weight_ref[...] = master_ref[...].astype(bf16)
    col_ref[...] = jnp.broadcast_to(gain_ref[...], (8, F)).T[:, 0:1]


def main_kernel(
    factor_ref, x_ref, got_ref, col_ref, weight_ref, gh_ref, gw_ref, inv_ref, send_ref, rows_ref, gx_ref
):
    total = jnp.zeros((4, 128), f32)
    for slot in range(TP):
        total = total + join_rows(got_ref[slot, 128:144, :])
        for c in range(8):
            rows_ref[slot * 16 : (slot + 1) * 16, c * 128 : (c + 1) * 128] = got_ref[
                slot, c * 16 : (c + 1) * 16, :
            ]
    inv = lax.rsqrt(as_row(total) * (1.0 / D) + 1e-05)
    inv_ref[...] = inv
    gx = x_ref[...] * col_ref[...]
    gx_ref[...] = (gx * inv).astype(bf16)
    parts = []
    for n in range(2):
        cols = slice(n * 256, (n + 1) * 256)
        gh = lax.dot_general(
            weight_ref[...], rows_ref[cols, :], (((1,), (1,)), ((), ())), preferred_element_type=f32
        )
        gh_ref[:, cols] = gh
        inner = jnp.sum(gx[:, cols] * gh, axis=0, keepdims=True)
        parts += [inner[:, 0:128], inner[:, 128:256]]
    factor = factor_ref[0]
    square = jnp.zeros((1, 256), f32)
    for n in range(4):
        cols = slice(n * 256, (n + 1) * 256)
        part = factor * jnp.dot(gx_ref[...], rows_ref[:, cols], preferred_element_type=f32)
        gw_ref[:, cols] = part
        square = square + jnp.sum(part * part, axis=0, keepdims=True)
    own_sq = jnp.broadcast_to(jnp.sum(square, axis=1, keepdims=True), (4, 128))
    packed = jnp.concatenate(parts + [own_sq], axis=0)
    for peer in range(TP):
        send_ref[peer] = packed


def terms_kernel(x_ref, gh_ref, inv_ref, col_ref, plain_ref, slope_ref):
    inv = inv_ref[...]
    plain_ref[...] = inv * (col_ref[...] * gh_ref[...])
    slope_ref[...] = x_ref[...] * (inv * inv * inv * (1.0 / D))


def branch_kernel(plain_ref, slope_ref, got_ref, send_ref, pin_ref):
    packed = got_ref[0]
    for peer in range(1, TP):
        packed = packed + got_ref[peer]
    pin_ref[...] = packed
    sent = (plain_ref[...] - slope_ref[...] * as_row(packed[0:4])).astype(bf16)
    layer_sq = split_rows(jnp.concatenate([packed[4:5]] * 4, axis=1))
    for j in range(SEC):
        for q in range(4):
            send_ref[j, q * 16 : (q + 1) * 16, :] = sent[j * 16 : (j + 1) * 16, q * 128 : (q + 1) * 128]
        send_ref[j, 64:80, :] = layer_sq


def decay_kernel(keep_ref, master_ref, pin_ref, out_ref):
    out_ref[...] = (keep_ref[0] * decay) * master_ref[...]


def suffix_kernel(got_ref, back_ref, clip_ref):
    running = jnp.zeros((64, 128), f32)
    norm = jnp.zeros((4, 128), f32)
    for s in range(SEC - 1, -1, -1):
        running = running + got_ref[s, 0:64, :].astype(f32)
        back_ref[s] = running.astype(bf16)
        norm = norm + join_rows(got_ref[s, 64:80, :])
    clip = jnp.minimum(1.0, clip_norm / (jnp.sqrt(norm) + 1e-06))
    clip_ref[...] = jnp.concatenate([clip, clip], axis=0)


def last_kernel(back_ref, out_ref):
    rows = []
    for j in range(SEC):
        rows.append(jnp.concatenate([back_ref[j, q * 16 : (q + 1) * 16, :] for q in range(4)], axis=1))
    out = jnp.concatenate(rows, axis=0).astype(f32).T.reshape(TP, 2, 8, F)
    for m in range(2):
        out_ref[m] = out[:, m].reshape(256, F).astype(bf16)


def on_device(hidden, gain, key_grad, master, moment, second, overflow):
    flag = overflow[0]
    factor = jnp.where(flag == 0, 1.0, jnp.where(flag == 1, 0.5, 0.0)).astype(f32)
    keep = jnp.where(flag == 2, 0.0, 1.0).astype(f32)

    xt, send = pl.pallas_call(
        first_kernel,
        out_shape=(sds((F, TOK)), sds((TP, 144, 128), bf16)),
        in_specs=[pl.BlockSpec(memory_space=pltpu.HBM)] * 2,
        out_specs=(VM, VM),
        scratch_shapes=[
            pltpu.VMEM((2, 256, F), bf16),
            pltpu.VMEM((16, K), bf16),
            pltpu.SemaphoreType.DMA((2,)),
        ],
        compiler_params=pltpu.CompilerParams(vmem_limit_bytes=32 * 1024 * 1024),
    )(hidden[0], key_grad.reshape(16, K))
    got = swap(send, "tp")
    weight, col = call(weight_kernel, (sds((F, K), bf16), sds((F, 1))), 3, 0, 3 * 512 * 1024)(
        master[0], gain, xt
    )
    gh, gw, inv, send = call(
        main_kernel,
        (sds((F, TOK)), sds((F, K)), sds((1, TOK)), sds((TP, 8, 128))),
        4,
        4 * F * TOK * K,
        4 * 1024 * 1024,
        [pltpu.VMEM((TOK, K), bf16), pltpu.VMEM((F, TOK), bf16)],
        1,
    )(factor[None], xt, got, col, weight)
    got = swap(send, "tp")
    plain, slope = call(terms_kernel, (sds((F, TOK)), sds((F, TOK))), 4, 6 * F * TOK, 2 * 1024 * 1024)(
        xt, gh, inv, col
    )
    send, pin = call(
        branch_kernel, (sds((SEC, 80, 128), bf16), sds((8, 128))), 3, 3 * F * TOK, 2 * 1024 * 1024
    )(plain, slope, got)
    got = swap(send, "section")
    decayed = call(decay_kernel, sds((F, K)), 2, F * K, 2 * 1024 * 1024, (), 1)(keep[None], master[0], pin)
    back, clip = call(
        suffix_kernel, (sds((SEC, 64, 128), bf16), sds((8, 128))), 1, 4 * F * TOK, 1024 * 1024
    )(got)
    back = swap(back, "section")
    clipped = clip[0, 0] * gw
    moment_new = beta_one * moment[0] + (1.0 - beta_one) * clipped
    second_new = beta_two * second[0] + (1.0 - beta_two) * clipped * clipped
    bias_one = 1.0 - beta_one**step_count
    bias_two = 1.0 - beta_two**step_count
    step = keep * (moment_new / bias_one / (jnp.sqrt(second_new / bias_two) + 1e-08)) + decayed
    grad_input = call(last_kernel, sds((2, 256, F), bf16), 1, F * TOK, 1024 * 1024)(back)
    return (grad_input[None], step[None])


def solution(mesh):
    return jax.shard_map(
        on_device,
        mesh=mesh,
        in_specs=(
            P("section", None, None, "tp"),
            P("section", "tp"),
            P("section", None, "tp", None),
            P("section", "tp", None),
            P("section", "tp", None),
            P("section", "tp", None),
            P("section"),
        ),
        out_specs=(P("section", None, None, "tp"), P("section", "tp", None)),
        check_vma=False,
    )
```

```python
import jax
import jax.numpy as jnp
from jax import lax
from jax.experimental import pallas as pl
from jax.experimental.pallas import tpu as pltpu
from jax.sharding import Mesh, PartitionSpec as P

D = 8192
SEC, NZ, NX = 16, 8, 4
TP = NZ * NX
TOK = 512
F = 256
K = 1024
f32, bf16 = jnp.float32, jnp.bfloat16

beta_one = 0.9
beta_two = 0.999
decay = 0.1
clip_norm = 1.0
step_count = 10

VM = pl.BlockSpec(memory_space=pltpu.VMEM)
SM = pl.BlockSpec(memory_space=pltpu.SMEM)


def call(body, out_shape, n_in, flops=0, data=0, scratch=(), scalars=0):
    outs = (VM,) * len(out_shape) if isinstance(out_shape, tuple) else VM
    return pl.pallas_call(
        body,
        out_shape=out_shape,
        in_specs=[SM] * scalars + [VM] * n_in,
        out_specs=outs,
        scratch_shapes=list(scratch),
        compiler_params=pltpu.CompilerParams(vmem_limit_bytes=32 * 1024 * 1024),
        cost_estimate=pl.CostEstimate(flops=flops, bytes_accessed=data, transcendentals=0),
    )


def sds(shape, dtype=f32):
    return jax.ShapeDtypeStruct(shape, dtype)


def swap(blocks, axis):
    return lax.all_to_all(blocks, axis, split_axis=0, concat_axis=0, tiled=True)


def split_rows(row):
    rows = jnp.concatenate([row[:, i * 128 : (i + 1) * 128] for i in range(4)], axis=0)
    high = rows.astype(bf16).astype(f32)
    low = rows - high
    return jnp.concatenate([high, low, jnp.zeros((8, 128), f32)], axis=0).astype(bf16)


def join_rows(rows):
    rows = rows.astype(f32)
    return rows[0:4] + rows[4:8]


def as_row(rows):
    return jnp.concatenate([rows[i : i + 1] for i in range(4)], axis=1)


def features_first(x_ref):
    x = x_ref[...].astype(f32).reshape(2, TP, 8, F)
    return jnp.concatenate([x[0][:, None], x[1][:, None]], axis=1).reshape(TOK, F).T


def first_kernel(x_ref, key_ref, send_ref):
    xt = features_first(x_ref)
    sums = split_rows(jnp.sum(xt * xt, axis=0, keepdims=True))
    for peer in range(NZ):
        for c in range(8):
            send_ref[peer, c * 16 : (c + 1) * 16, :] = key_ref[:, c * 128 : (c + 1) * 128]
        send_ref[peer, 128:144, :] = sums


def middle_kernel(got_ref, send_ref):
    total = jnp.zeros((4, 128), f32)
    for z in range(NZ):
        total = total + join_rows(got_ref[z, 128:144, :])
    sums = split_rows(as_row(total))
    for peer in range(NX):
        for z in range(NZ):
            send_ref[peer, z * 128 : (z + 1) * 128, :] = got_ref[z, 0:128, :]
        send_ref[peer, 1024:1040, :] = sums


def main_kernel(
    factor_ref, x_ref, got_ref, gain_ref, master_ref, gw_ref, plain_ref, slope_ref, send_ref, rows_ref, gx_ref
):
    for x in range(NX):
        for z in range(NZ):
            slot = z * NX + x
            for c in range(8):
                rows_ref[slot * 16 : (slot + 1) * 16, c * 128 : (c + 1) * 128] = got_ref[
                    x, z * 128 + c * 16 : z * 128 + (c + 1) * 16, :
                ]
    total = jnp.zeros((4, 128), f32)
    for x in range(NX):
        total = total + join_rows(got_ref[x, 1024:1040, :])
    inv = lax.rsqrt(as_row(total) * (1.0 / D) + 1e-05)
    col = jnp.broadcast_to(gain_ref[...], (8, F)).T[:, 0:1]
    xt = features_first(x_ref)
    gx = xt * col
    gx_ref[...] = (gx * inv).astype(bf16)
    slope_ref[...] = xt * (inv * inv * inv * (1.0 / D))
    factor = factor_ref[0]
    square = jnp.zeros((1, 256), f32)
    for n in range(4):
        cols = slice(n * 256, (n + 1) * 256)
        part = factor * jnp.dot(gx_ref[...], rows_ref[:, cols], preferred_element_type=f32)
        gw_ref[:, cols] = part
        square = square + jnp.sum(part * part, axis=0, keepdims=True)
    own_sq = jnp.broadcast_to(jnp.sum(square, axis=1, keepdims=True), (4, 128))
    weight = master_ref[...].astype(bf16)
    parts = []
    for n in range(2):
        cols = slice(n * 256, (n + 1) * 256)
        gh = lax.dot_general(
            weight, rows_ref[cols, :], (((1,), (1,)), ((), ())), preferred_element_type=f32
        )
        plain_ref[:, cols] = inv[:, cols] * (col * gh)
        inner = jnp.sum(gx[:, cols] * gh, axis=0, keepdims=True)
        parts += [inner[:, 0:128], inner[:, 128:256]]
    packed = jnp.concatenate(parts + [own_sq], axis=0)
    for peer in range(TP):
        send_ref[peer] = packed


def branch_kernel(plain_ref, slope_ref, got_ref, send_ref):
    packed = got_ref[0]
    for peer in range(1, TP):
        packed = packed + got_ref[peer]
    sent = (plain_ref[...] - slope_ref[...] * as_row(packed[0:4])).astype(bf16)
    layer_sq = split_rows(jnp.concatenate([packed[4:5]] * 4, axis=1))
    for j in range(SEC):
        for q in range(4):
            send_ref[j, q * 16 : (q + 1) * 16, :] = sent[j * 16 : (j + 1) * 16, q * 128 : (q + 1) * 128]
        send_ref[j, 64:72, :] = layer_sq[0:8]


def suffix_kernel(got_ref, back_ref, clip_ref):
    running = jnp.zeros((64, 128), f32)
    norm = jnp.zeros((4, 128), f32)
    for s in range(SEC - 1, -1, -1):
        running = running + got_ref[s, 0:64, :].astype(f32)
        back_ref[s] = running.astype(bf16)
        norm = norm + join_rows(got_ref[s, 64:72, :])
    clip = jnp.minimum(1.0, clip_norm / (jnp.sqrt(norm) + 1e-06))
    clip_ref[...] = jnp.concatenate([clip, clip], axis=0)


def last_kernel(back_ref, out_ref):
    rows = []
    for j in range(SEC):
        rows.append(jnp.concatenate([back_ref[j, q * 16 : (q + 1) * 16, :] for q in range(4)], axis=1))
    out = jnp.concatenate(rows, axis=0).astype(f32).T.reshape(TP, 2, 8, F)
    for m in range(2):
        out_ref[m] = out[:, m].reshape(256, F).astype(bf16)


def on_device(hidden, gain, key_grad, master, moment, second, overflow):
    flag = overflow[0]
    factor = jnp.where(flag == 0, 1.0, jnp.where(flag == 1, 0.5, 0.0)).astype(f32)
    keep = jnp.where(flag == 2, 0.0, 1.0).astype(f32)

    send = call(first_kernel, sds((NZ, 144, 128), bf16), 2, 3 * F * TOK, F * TOK * 2)(
        hidden[0], key_grad.reshape(16, K)
    )
    got = swap(send, "z")
    send = call(middle_kernel, sds((NX, 1040, 128), bf16), 1, 0, 1024 * 1024)(got)
    got = swap(send, "x")
    gw, plain, slope, send = call(
        main_kernel,
        (sds((F, K)), sds((F, TOK)), sds((F, TOK)), sds((TP, 8, 128))),
        4,
        4 * F * TOK * K,
        4 * 1024 * 1024,
        [pltpu.VMEM((TOK, K), bf16), pltpu.VMEM((F, TOK), bf16)],
        1,
    )(factor[None], hidden[0], got, gain, master[0])
    got = swap(send, ("z", "x"))
    send = call(branch_kernel, sds((SEC, 72, 128), bf16), 3, 3 * F * TOK, 1024 * 1024)(plain, slope, got)
    got = swap(send, ("y", "core"))
    back, clip = call(
        suffix_kernel, (sds((SEC, 64, 128), bf16), sds((8, 128))), 1, 4 * F * TOK, 1024 * 1024
    )(got)
    back = swap(back, ("y", "core"))
    clipped = clip[0, 0] * gw
    moment_new = beta_one * moment[0] + (1.0 - beta_one) * clipped
    second_new = beta_two * second[0] + (1.0 - beta_two) * clipped * clipped
    bias_one = 1.0 - beta_one**step_count
    bias_two = 1.0 - beta_two**step_count
    update = moment_new / bias_one / (jnp.sqrt(second_new / bias_two) + 1e-08) + decay * master[0]
    grad_input = call(last_kernel, sds((2, 256, F), bf16), 1, F * TOK, 1024 * 1024)(back)
    return (grad_input[None], (keep * update)[None])


def solution(mesh):
    fine = Mesh(mesh.devices.reshape(8, 2, NZ, NX), ("y", "core", "z", "x"))
    sec, tp = ("y", "core"), ("z", "x")
    return jax.shard_map(
        on_device,
        mesh=fine,
        in_specs=(
            P(sec, None, None, tp),
            P(sec, tp),
            P(sec, None, tp, None),
            P(sec, tp, None),
            P(sec, tp, None),
            P(sec, tp, None),
            P(sec),
        ),
        out_specs=(P(sec, None, None, tp), P(sec, tp, None)),
        check_vma=False,
    )
```

```python
import jax
import jax.numpy as jnp
from jax import lax
from jax.experimental import pallas as pl
from jax.experimental.pallas import tpu as pltpu
from jax.sharding import Mesh, PartitionSpec as P

D = 8192
SEC, NZ, NX = 16, 8, 4
TP = NZ * NX
TOK = 512
F = 256
K = 1024
f32, bf16 = jnp.float32, jnp.bfloat16

beta_one = 0.9
beta_two = 0.999
decay = 0.1
clip_norm = 1.0
step_count = 10

VM = pl.BlockSpec(memory_space=pltpu.VMEM)
SM = pl.BlockSpec(memory_space=pltpu.SMEM)


def call(body, out_shape, n_in, flops=0, data=0, scratch=(), scalars=0):
    outs = (VM,) * len(out_shape) if isinstance(out_shape, tuple) else VM
    return pl.pallas_call(
        body,
        out_shape=out_shape,
        in_specs=[SM] * scalars + [VM] * n_in,
        out_specs=outs,
        scratch_shapes=list(scratch),
        compiler_params=pltpu.CompilerParams(vmem_limit_bytes=32 * 1024 * 1024),
        cost_estimate=pl.CostEstimate(flops=flops, bytes_accessed=data, transcendentals=0),
    )


def sds(shape, dtype=f32):
    return jax.ShapeDtypeStruct(shape, dtype)


def swap(blocks, axis):
    return lax.all_to_all(blocks, axis, split_axis=0, concat_axis=0, tiled=True)


def shift(value, k):
    return lax.ppermute(value, "x", [(x, (x + k) % NX) for x in range(NX)])


def split_rows(row):
    rows = jnp.concatenate([row[:, i * 128 : (i + 1) * 128] for i in range(4)], axis=0)
    high = rows.astype(bf16).astype(f32)
    low = rows - high
    return jnp.concatenate([high, low, jnp.zeros((8, 128), f32)], axis=0).astype(bf16)


def join_rows(rows):
    rows = rows.astype(f32)
    return rows[0:4] + rows[4:8]


def as_row(rows):
    return jnp.concatenate([rows[i : i + 1] for i in range(4)], axis=1)


def features_first(x_ref):
    x = x_ref[...].astype(f32).reshape(2, TP, 8, F)
    return jnp.concatenate([x[0][:, None], x[1][:, None]], axis=1).reshape(TOK, F).T


def first_kernel(x_ref, key_ref, send_ref):
    xt = features_first(x_ref)
    sums = split_rows(jnp.sum(xt * xt, axis=0, keepdims=True))
    for peer in range(NZ):
        for c in range(8):
            send_ref[peer, c * 16 : (c + 1) * 16, :] = key_ref[:, c * 128 : (c + 1) * 128]
        send_ref[peer, 128:144, :] = sums


def middle_kernel(got_ref, send_ref):
    total = jnp.zeros((4, 128), f32)
    for z in range(NZ):
        total = total + join_rows(got_ref[z, 128:144, :])
    sums = split_rows(as_row(total))
    for z in range(NZ):
        send_ref[z * 128 : (z + 1) * 128, :] = got_ref[z, 0:128, :]
    send_ref[1024:1040, :] = sums


def main_kernel(
    factor_ref, at_ref, x_ref, got0, got1, got2, got3, gain_ref, master_ref,
    gw_ref, plain_ref, slope_ref, send_ref, rows_ref, gx_ref,
):
    total = jnp.zeros((4, 128), f32)
    for back, got_ref in enumerate((got0, got1, got2, got3)):
        column = (at_ref[0] + NX - back) % NX
        for z in range(NZ):
            start = pl.multiple_of((z * NX + column) * 16, 16)
            for c in range(8):
                rows_ref[pl.ds(start, 16), c * 128 : (c + 1) * 128] = got_ref[
                    z * 128 + c * 16 : z * 128 + (c + 1) * 16, :
                ]
        total = total + join_rows(got_ref[1024:1040, :])
    inv = lax.rsqrt(as_row(total) * (1.0 / D) + 1e-05)
    col = jnp.broadcast_to(gain_ref[...], (8, F)).T[:, 0:1]
    xt = features_first(x_ref)
    gx = xt * col
    gx_ref[...] = (gx * inv).astype(bf16)
    slope_ref[...] = xt * (inv * inv * inv * (1.0 / D))
    factor = factor_ref[0]
    square = jnp.zeros((1, 256), f32)
    for n in range(4):
        cols = slice(n * 256, (n + 1) * 256)
        part = factor * jnp.dot(gx_ref[...], rows_ref[:, cols], preferred_element_type=f32)
        gw_ref[:, cols] = part
        square = square + jnp.sum(part * part, axis=0, keepdims=True)
    own_sq = jnp.broadcast_to(jnp.sum(square, axis=1, keepdims=True), (4, 128))
    weight = master_ref[...].astype(bf16)
    parts = []
    for n in range(2):
        cols = slice(n * 256, (n + 1) * 256)
        gh = lax.dot_general(
            weight, rows_ref[cols, :], (((1,), (1,)), ((), ())), preferred_element_type=f32
        )
        plain_ref[:, cols] = inv[:, cols] * (col * gh)
        inner = jnp.sum(gx[:, cols] * gh, axis=0, keepdims=True)
        parts += [inner[:, 0:128], inner[:, 128:256]]
    packed = jnp.concatenate(parts + [own_sq], axis=0)
    for peer in range(TP):
        send_ref[peer] = packed


def branch_kernel(plain_ref, slope_ref, got_ref, send_ref):
    packed = got_ref[0]
    for peer in range(1, TP):
        packed = packed + got_ref[peer]
    sent = (plain_ref[...] - slope_ref[...] * as_row(packed[0:4])).astype(bf16)
    layer_sq = split_rows(jnp.concatenate([packed[4:5]] * 4, axis=1))
    for j in range(SEC):
        for q in range(4):
            send_ref[j, q * 16 : (q + 1) * 16, :] = sent[j * 16 : (j + 1) * 16, q * 128 : (q + 1) * 128]
        send_ref[j, 64:72, :] = layer_sq[0:8]


def suffix_kernel(got_ref, back_ref, clip_ref):
    running = jnp.zeros((64, 128), f32)
    norm = jnp.zeros((4, 128), f32)
    for s in range(SEC - 1, -1, -1):
        running = running + got_ref[s, 0:64, :].astype(f32)
        back_ref[s] = running.astype(bf16)
        norm = norm + join_rows(got_ref[s, 64:72, :])
    clip = jnp.minimum(1.0, clip_norm / (jnp.sqrt(norm) + 1e-06))
    clip_ref[...] = jnp.concatenate([clip, clip], axis=0)


def last_kernel(back_ref, out_ref):
    rows = []
    for j in range(SEC):
        rows.append(jnp.concatenate([back_ref[j, q * 16 : (q + 1) * 16, :] for q in range(4)], axis=1))
    out = jnp.concatenate(rows, axis=0).astype(f32).T.reshape(TP, 2, 8, F)
    for m in range(2):
        out_ref[m] = out[:, m].reshape(256, F).astype(bf16)


def on_device(hidden, gain, key_grad, master, moment, second, overflow):
    flag = overflow[0]
    factor = jnp.where(flag == 0, 1.0, jnp.where(flag == 1, 0.5, 0.0)).astype(f32)
    keep = jnp.where(flag == 2, 0.0, 1.0).astype(f32)

    send = call(first_kernel, sds((NZ, 144, 128), bf16), 2, 3 * F * TOK, F * TOK * 2)(
        hidden[0], key_grad.reshape(16, K)
    )
    got = swap(send, "z")
    own = call(middle_kernel, sds((1040, 128), bf16), 1, 0, 512 * 1024)(got)
    got1 = shift(own, 1)
    got3 = shift(own, 3)
    got2 = shift(own, 2)
    at = lax.axis_index("x").astype(jnp.int32)
    gw, plain, slope, send = call(
        main_kernel,
        (sds((F, K)), sds((F, TOK)), sds((F, TOK)), sds((TP, 8, 128))),
        7,
        4 * F * TOK * K,
        4 * 1024 * 1024,
        [pltpu.VMEM((TOK, K), bf16), pltpu.VMEM((F, TOK), bf16)],
        2,
    )(factor[None], at[None], hidden[0], own, got1, got2, got3, gain, master[0])
    got = swap(send, ("z", "x"))
    send = call(branch_kernel, sds((SEC, 72, 128), bf16), 3, 3 * F * TOK, 1024 * 1024)(plain, slope, got)
    got = swap(send, ("y", "core"))
    back, clip = call(
        suffix_kernel, (sds((SEC, 64, 128), bf16), sds((8, 128))), 1, 4 * F * TOK, 1024 * 1024
    )(got)
    back = swap(back, ("y", "core"))
    clipped = clip[0, 0] * gw
    moment_new = beta_one * moment[0] + (1.0 - beta_one) * clipped
    second_new = beta_two * second[0] + (1.0 - beta_two) * clipped * clipped
    bias_one = 1.0 - beta_one**step_count
    bias_two = 1.0 - beta_two**step_count
    update = moment_new / bias_one / (jnp.sqrt(second_new / bias_two) + 1e-08) + decay * master[0]
    grad_input = call(last_kernel, sds((2, 256, F), bf16), 1, F * TOK, 1024 * 1024)(back)
    return (grad_input[None], (keep * update)[None])


def solution(mesh):
    fine = Mesh(mesh.devices.reshape(8, 2, NZ, NX), ("y", "core", "z", "x"))
    sec, tp = ("y", "core"), ("z", "x")
    return jax.shard_map(
        on_device,
        mesh=fine,
        in_specs=(
            P(sec, None, None, tp),
            P(sec, tp),
            P(sec, None, tp, None),
            P(sec, tp, None),
            P(sec, tp, None),
            P(sec, tp, None),
            P(sec),
        ),
        out_specs=(P(sec, None, None, tp), P(sec, tp, None)),
        check_vma=False,
    )
```

```python
import jax
import jax.numpy as jnp
from jax import lax
from jax.experimental import pallas as pl
from jax.experimental.pallas import tpu as pltpu
from jax.sharding import Mesh, PartitionSpec as P

D = 8192
SEC, NZ, NX = 16, 8, 4
TP = NZ * NX
TOK = 512
F = 256
K = 1024
f32, bf16 = jnp.float32, jnp.bfloat16

beta_one = 0.9
beta_two = 0.999
decay = 0.1
clip_norm = 1.0
step_count = 10

VM = pl.BlockSpec(memory_space=pltpu.VMEM)
SM = pl.BlockSpec(memory_space=pltpu.SMEM)


def call(body, out_shape, n_in, flops=0, data=0, scratch=(), scalars=0):
    outs = (VM,) * len(out_shape) if isinstance(out_shape, tuple) else VM
    return pl.pallas_call(
        body,
        out_shape=out_shape,
        in_specs=[SM] * scalars + [VM] * n_in,
        out_specs=outs,
        scratch_shapes=list(scratch),
        compiler_params=pltpu.CompilerParams(vmem_limit_bytes=32 * 1024 * 1024),
        cost_estimate=pl.CostEstimate(flops=flops, bytes_accessed=data, transcendentals=0),
    )


def sds(shape, dtype=f32):
    return jax.ShapeDtypeStruct(shape, dtype)


def swap(blocks, axis):
    return lax.all_to_all(blocks, axis, split_axis=0, concat_axis=0, tiled=True)


def split_rows(row):
    rows = jnp.concatenate([row[:, i * 128 : (i + 1) * 128] for i in range(4)], axis=0)
    high = rows.astype(bf16).astype(f32)
    low = rows - high
    return jnp.concatenate([high, low, jnp.zeros((8, 128), f32)], axis=0).astype(bf16)


def join_rows(rows):
    rows = rows.astype(f32)
    return rows[0:4] + rows[4:8]


def as_row(rows):
    return jnp.concatenate([rows[i : i + 1] for i in range(4)], axis=1)


def tokens_first(x_ref):
    x = x_ref[...].astype(f32).reshape(2, TP, 8, F)
    return jnp.concatenate([x[0][:, None], x[1][:, None]], axis=1).reshape(TOK, F)


def column(row):
    return jnp.broadcast_to(row, (8, row.shape[1])).T[:, 0:1]


def first_kernel(x_ref, key_ref, send_ref):
    xt = tokens_first(x_ref).T
    sums = split_rows(jnp.sum(xt * xt, axis=0, keepdims=True))
    for peer in range(NZ):
        for c in range(8):
            send_ref[peer, c * 16 : (c + 1) * 16, :] = key_ref[:, c * 128 : (c + 1) * 128]
        send_ref[peer, 128:144, :] = sums


def middle_kernel(got_ref, send_ref):
    total = jnp.zeros((4, 128), f32)
    for z in range(NZ):
        total = total + join_rows(got_ref[z, 128:144, :])
    sums = split_rows(as_row(total))
    for peer in range(NX):
        for z in range(NZ):
            send_ref[peer, z * 128 : (z + 1) * 128, :] = got_ref[z, 0:128, :]
        send_ref[peer, 1024:1040, :] = sums


def main_kernel(
    flag_ref, x_ref, got_ref, gain_ref, master_ref, gw_ref, plain_ref, slope_ref, send_ref, rows_ref, gx_ref
):
    for x in range(NX):
        for z in range(NZ):
            slot = z * NX + x
            for c in range(8):
                rows_ref[slot * 16 : (slot + 1) * 16, c * 128 : (c + 1) * 128] = got_ref[
                    x, z * 128 + c * 16 : z * 128 + (c + 1) * 16, :
                ]
    total = jnp.zeros((4, 128), f32)
    for x in range(NX):
        total = total + join_rows(got_ref[x, 1024:1040, :])
    inv = lax.rsqrt(as_row(total) * (1.0 / D) + 1e-05)
    inv_col = column(inv)
    gain = gain_ref[...]
    x = tokens_first(x_ref)
    gx_ref[...] = (x.T * column(gain) * inv).astype(bf16)
    slope_ref[...] = x * (inv_col * inv_col * inv_col * (1.0 / D))
    gx = x * gain
    flag = flag_ref[...]
    factor = jnp.where(flag == 0, 1.0, jnp.where(flag == 1, 0.5, 0.0)).astype(f32)
    square = jnp.zeros((1, 256), f32)
    for n in range(4):
        cols = slice(n * 256, (n + 1) * 256)
        part = factor * jnp.dot(gx_ref[...], rows_ref[:, cols], preferred_element_type=f32)
        gw_ref[:, cols] = part
        square = square + jnp.sum(part * part, axis=0, keepdims=True)
    own_sq = jnp.broadcast_to(jnp.sum(square, axis=1, keepdims=True), (1, 128))
    weight = master_ref[...].astype(bf16)
    parts = []
    for n in range(2):
        here = slice(n * 256, (n + 1) * 256)
        gh = lax.dot_general(
            rows_ref[here, :], weight, (((1,), (1,)), ((), ())), preferred_element_type=f32
        )
        plain_ref[here, :] = inv_col[here] * (gain * gh)
        inner = jnp.sum(gx[here] * gh, axis=1, keepdims=True)
        parts.append(jnp.broadcast_to(inner, (256, 128)).T[0:1, :])
    packed = jnp.concatenate(parts + [own_sq], axis=1)
    for peer in range(TP):
        send_ref[peer] = packed


def branch_kernel(plain_ref, slope_ref, got_ref, send_ref):
    packed = got_ref[0]
    for peer in range(1, TP):
        packed = packed + got_ref[peer]
    branch = plain_ref[...] - slope_ref[...] * column(packed[:, 0:TOK])
    branch = branch.reshape(TP, 2, 8, F)
    layer_sq = split_rows(jnp.concatenate([packed[:, TOK:]] * 4, axis=1))
    for m in range(2):
        sent = branch[:, m].reshape(256, F).astype(bf16)
        for i in range(8):
            j = m * 8 + i
            send_ref[j, 0:32, :] = sent[i * 32 : (i + 1) * 32, 0:128]
            send_ref[j, 32:64, :] = sent[i * 32 : (i + 1) * 32, 128:256]
            send_ref[j, 64:72, :] = layer_sq[0:8]


def suffix_kernel(got_ref, flag_ref, back_ref, clip_ref):
    running = jnp.zeros((64, 128), f32)
    norm = jnp.zeros((4, 128), f32)
    for s in range(SEC - 1, -1, -1):
        running = running + got_ref[s, 0:64, :].astype(f32)
        sums = running.astype(bf16)
        back_ref[s, :, 0:128] = sums[0:32]
        back_ref[s, :, 128:256] = sums[32:64]
        norm = norm + join_rows(got_ref[s, 64:72, :])
    clip = jnp.minimum(1.0, clip_norm / (jnp.sqrt(norm) + 1e-06))
    keep = jnp.broadcast_to(jnp.where(flag_ref[...] == 2, 0.0, 1.0).astype(f32), (4, 128))
    clip_ref[...] = jnp.concatenate([clip, keep], axis=0)


def on_device(hidden, gain, key_grad, master, moment, second, overflow):
    flag = overflow.reshape(1, 1)
    send = call(first_kernel, sds((NZ, 144, 128), bf16), 2, 0, 0)(hidden[0], key_grad.reshape(16, K))
    got = swap(send, "z")
    send = call(middle_kernel, sds((NX, 1040, 128), bf16), 1, 0, 1024 * 1024)(got)
    got = swap(send, "x")
    gw, plain, slope, send = call(
        main_kernel,
        (sds((F, K)), sds((TOK, F)), sds((TOK, F)), sds((TP, 1, TOK + 128))),
        5,
        4 * F * TOK * K,
        4 * 1024 * 1024,
        [pltpu.VMEM((TOK, K), bf16), pltpu.VMEM((F, TOK), bf16)],
    )(flag, hidden[0], got, gain, master[0])
    got = swap(send, ("z", "x"))
    send = call(branch_kernel, sds((SEC, 72, 128), bf16), 3, 3 * F * TOK, 1024 * 1024)(plain, slope, got)
    got = swap(send, ("y", "core"))
    back, clip = call(
        suffix_kernel, (sds((SEC, 32, F), bf16), sds((8, 128))), 2, 4 * F * TOK, 1024 * 1024
    )(got, flag)
    back = swap(back, ("y", "core"))
    clipped = clip[0, 0] * gw
    moment_new = beta_one * moment[0] + (1.0 - beta_one) * clipped
    second_new = beta_two * second[0] + (1.0 - beta_two) * clipped * clipped
    bias_one = 1.0 - beta_one**step_count
    bias_two = 1.0 - beta_two**step_count
    update = moment_new / bias_one / (jnp.sqrt(second_new / bias_two) + 1e-08) + decay * master[0]
    keep = clip[4, 0]
    return (back.reshape(1, 2, 256, F), (keep * update)[None])


def solution(mesh):
    fine = Mesh(mesh.devices.reshape(8, 2, NZ, NX), ("y", "core", "z", "x"))
    sec, tp = ("y", "core"), ("z", "x")
    return jax.shard_map(
        on_device,
        mesh=fine,
        in_specs=(
            P(sec, None, None, tp),
            P(sec, tp),
            P(sec, None, tp, None),
            P(sec, tp, None),
            P(sec, tp, None),
            P(sec, tp, None),
            P(sec),
        ),
        out_specs=(P(sec, None, None, tp), P(sec, tp, None)),
        check_vma=False,
    )
```

```python
import jax
import jax.numpy as jnp
from jax import lax
from jax.experimental import pallas as pl
from jax.experimental.pallas import tpu as pltpu
from jax.sharding import Mesh, PartitionSpec as P

D = 8192
SEC, NZ, NX = 16, 8, 4
TP = NZ * NX
TOK = 512
F = 256
K = 1024
f32, bf16 = jnp.float32, jnp.bfloat16

beta_one = 0.9
beta_two = 0.999
decay = 0.1
clip_norm = 1.0
step_count = 10

VM = pl.BlockSpec(memory_space=pltpu.VMEM)
SM = pl.BlockSpec(memory_space=pltpu.SMEM)


def call(body, out_shape, n_in, flops=0, data=0, scratch=(), scalars=0):
    outs = (VM,) * len(out_shape) if isinstance(out_shape, tuple) else VM
    return pl.pallas_call(
        body,
        out_shape=out_shape,
        in_specs=[SM] * scalars + [VM] * n_in,
        out_specs=outs,
        scratch_shapes=list(scratch),
        compiler_params=pltpu.CompilerParams(vmem_limit_bytes=32 * 1024 * 1024),
        cost_estimate=pl.CostEstimate(flops=flops, bytes_accessed=data, transcendentals=0),
    )


def sds(shape, dtype=f32):
    return jax.ShapeDtypeStruct(shape, dtype)


def swap(blocks, axis):
    return lax.all_to_all(blocks, axis, split_axis=0, concat_axis=0, tiled=True)


def split_rows(row):
    rows = jnp.concatenate([row[:, i * 128 : (i + 1) * 128] for i in range(4)], axis=0)
    high = rows.astype(bf16).astype(f32)
    low = rows - high
    return jnp.concatenate([high, low, jnp.zeros((8, 128), f32)], axis=0).astype(bf16)


def join_rows(rows):
    rows = rows.astype(f32)
    return rows[0:4] + rows[4:8]


def as_row(rows):
    return jnp.concatenate([rows[i : i + 1] for i in range(4)], axis=1)


def tokens_first(x_ref):
    x = x_ref[...].astype(f32).reshape(2, TP, 8, F)
    return jnp.concatenate([x[0][:, None], x[1][:, None]], axis=1).reshape(TOK, F)


def column(row):
    return jnp.broadcast_to(row, (8, row.shape[1])).T[:, 0:1]


def first_kernel(x_ref, key_ref, send_ref):
    xt = tokens_first(x_ref).T
    sums = split_rows(jnp.sum(xt * xt, axis=0, keepdims=True))
    for c in range(8):
        send_ref[c * 16 : (c + 1) * 16, :] = key_ref[:, c * 128 : (c + 1) * 128]
    send_ref[128:144, :] = sums


def main_kernel(
    flag_ref, x_ref, got_ref, gain_ref, master_ref, gw_ref, plain_ref, slope_ref, send_ref, rows_ref, gx_ref
):
    total = jnp.zeros((4, 128), f32)
    for slot in range(TP):
        for c in range(8):
            rows_ref[slot * 16 : (slot + 1) * 16, c * 128 : (c + 1) * 128] = got_ref[
                slot, c * 16 : (c + 1) * 16, :
            ]
        total = total + join_rows(got_ref[slot, 128:144, :])
    inv = lax.rsqrt(as_row(total) * (1.0 / D) + 1e-05)
    inv_col = column(inv)
    gain = gain_ref[...]
    x = tokens_first(x_ref)
    gx_ref[...] = (x.T * column(gain) * inv).astype(bf16)
    slope_ref[...] = x * (inv_col * inv_col * inv_col * (1.0 / D))
    gx = x * gain
    flag = flag_ref[...]
    factor = jnp.where(flag == 0, 1.0, jnp.where(flag == 1, 0.5, 0.0)).astype(f32)
    square = jnp.zeros((1, 256), f32)
    for n in range(4):
        cols = slice(n * 256, (n + 1) * 256)
        part = factor * jnp.dot(gx_ref[...], rows_ref[:, cols], preferred_element_type=f32)
        gw_ref[:, cols] = part
        square = square + jnp.sum(part * part, axis=0, keepdims=True)
    own_sq = jnp.broadcast_to(jnp.sum(square, axis=1, keepdims=True), (1, 128))
    weight = master_ref[...].astype(bf16)
    parts = []
    for n in range(2):
        here = slice(n * 256, (n + 1) * 256)
        gh = lax.dot_general(
            rows_ref[here, :], weight, (((1,), (1,)), ((), ())), preferred_element_type=f32
        )
        plain_ref[here, :] = inv_col[here] * (gain * gh)
        inner = jnp.sum(gx[here] * gh, axis=1, keepdims=True)
        parts.append(jnp.broadcast_to(inner, (256, 128)).T[0:1, :])
    packed = jnp.concatenate(parts + [own_sq], axis=1)
    for peer in range(TP):
        send_ref[peer] = packed


def branch_kernel(plain_ref, slope_ref, got_ref, send_ref):
    packed = got_ref[0]
    for peer in range(1, TP):
        packed = packed + got_ref[peer]
    branch = plain_ref[...] - slope_ref[...] * column(packed[:, 0:TOK])
    branch = branch.reshape(TP, 2, 8, F)
    layer_sq = split_rows(jnp.concatenate([packed[:, TOK:]] * 4, axis=1))
    for m in range(2):
        sent = branch[:, m].reshape(256, F).astype(bf16)
        for i in range(8):
            j = m * 8 + i
            send_ref[j, 0:32, :] = sent[i * 32 : (i + 1) * 32, 0:128]
            send_ref[j, 32:64, :] = sent[i * 32 : (i + 1) * 32, 128:256]
            send_ref[j, 64:72, :] = layer_sq[0:8]


def suffix_kernel(got_ref, flag_ref, back_ref, clip_ref):
    running = jnp.zeros((64, 128), f32)
    norm = jnp.zeros((4, 128), f32)
    for s in range(SEC - 1, -1, -1):
        running = running + got_ref[s, 0:64, :].astype(f32)
        sums = running.astype(bf16)
        back_ref[s, :, 0:128] = sums[0:32]
        back_ref[s, :, 128:256] = sums[32:64]
        norm = norm + join_rows(got_ref[s, 64:72, :])
    clip = jnp.minimum(1.0, clip_norm / (jnp.sqrt(norm) + 1e-06))
    keep = jnp.broadcast_to(jnp.where(flag_ref[...] == 2, 0.0, 1.0).astype(f32), (4, 128))
    clip_ref[...] = jnp.concatenate([clip, keep], axis=0)


def on_device(hidden, gain, key_grad, master, moment, second, overflow):
    flag = overflow.reshape(1, 1)
    send = call(first_kernel, sds((144, 128), bf16), 2, 0, 0)(hidden[0], key_grad.reshape(16, K))
    got = lax.all_gather(send, ("z", "x"))
    gw, plain, slope, send = call(
        main_kernel,
        (sds((F, K)), sds((TOK, F)), sds((TOK, F)), sds((TP, 1, TOK + 128))),
        5,
        4 * F * TOK * K,
        4 * 1024 * 1024,
        [pltpu.VMEM((TOK, K), bf16), pltpu.VMEM((F, TOK), bf16)],
    )(flag, hidden[0], got, gain, master[0])
    got = swap(send, ("z", "x"))
    send = call(branch_kernel, sds((SEC, 72, 128), bf16), 3, 3 * F * TOK, 1024 * 1024)(plain, slope, got)
    got = swap(send, ("y", "core"))
    back, clip = call(
        suffix_kernel, (sds((SEC, 32, F), bf16), sds((8, 128))), 2, 4 * F * TOK, 1024 * 1024
    )(got, flag)
    back = swap(back, ("y", "core"))
    clipped = clip[0, 0] * gw
    moment_new = beta_one * moment[0] + (1.0 - beta_one) * clipped
    second_new = beta_two * second[0] + (1.0 - beta_two) * clipped * clipped
    bias_one = 1.0 - beta_one**step_count
    bias_two = 1.0 - beta_two**step_count
    update = moment_new / bias_one / (jnp.sqrt(second_new / bias_two) + 1e-08) + decay * master[0]
    keep = clip[4, 0]
    return (back.reshape(1, 2, 256, F), (keep * update)[None])


def solution(mesh):
    fine = Mesh(mesh.devices.reshape(8, 2, NZ, NX), ("y", "core", "z", "x"))
    sec, tp = ("y", "core"), ("z", "x")
    return jax.shard_map(
        on_device,
        mesh=fine,
        in_specs=(
            P(sec, None, None, tp),
            P(sec, tp),
            P(sec, None, tp, None),
            P(sec, tp, None),
            P(sec, tp, None),
            P(sec, tp, None),
            P(sec),
        ),
        out_specs=(P(sec, None, None, tp), P(sec, tp, None)),
        check_vma=False,
    )
```

```python
import jax
import jax.numpy as jnp
from jax import lax
from jax.experimental import pallas as pl
from jax.experimental.pallas import tpu as pltpu
from jax.sharding import Mesh, PartitionSpec as P

D = 8192
SEC, NZ, NX = 16, 8, 4
TP = NZ * NX
TOK = 512
F = 256
K = 1024
f32, bf16 = jnp.float32, jnp.bfloat16

beta_one = 0.9
beta_two = 0.999
decay = 0.1
clip_norm = 1.0
step_count = 10

VM = pl.BlockSpec(memory_space=pltpu.VMEM)
SM = pl.BlockSpec(memory_space=pltpu.SMEM)


def call(body, out_shape, n_in, flops=0, data=0, scratch=(), scalars=0):
    outs = (VM,) * len(out_shape) if isinstance(out_shape, tuple) else VM
    return pl.pallas_call(
        body,
        out_shape=out_shape,
        in_specs=[SM] * scalars + [VM] * n_in,
        out_specs=outs,
        scratch_shapes=list(scratch),
        compiler_params=pltpu.CompilerParams(vmem_limit_bytes=32 * 1024 * 1024),
        cost_estimate=pl.CostEstimate(flops=flops, bytes_accessed=data, transcendentals=0),
    )


def sds(shape, dtype=f32):
    return jax.ShapeDtypeStruct(shape, dtype)


def swap(blocks, axis):
    return lax.all_to_all(blocks, axis, split_axis=0, concat_axis=0, tiled=True)


def split_rows(row):
    rows = jnp.concatenate([row[:, i * 128 : (i + 1) * 128] for i in range(4)], axis=0)
    high = rows.astype(bf16).astype(f32)
    low = rows - high
    return jnp.concatenate([high, low, jnp.zeros((8, 128), f32)], axis=0).astype(bf16)


def join_rows(rows):
    rows = rows.astype(f32)
    return rows[0:4] + rows[4:8]


def as_row(rows):
    return jnp.concatenate([rows[i : i + 1] for i in range(4)], axis=1)


def features_first(x_ref):
    x = x_ref[...].astype(f32).reshape(2, TP, 8, F)
    return jnp.concatenate([x[0][:, None], x[1][:, None]], axis=1).reshape(TOK, F).T


def first_kernel(x_ref, key_ref, send_ref):
    xt = features_first(x_ref)
    sums = split_rows(jnp.sum(xt * xt, axis=0, keepdims=True))
    for peer in range(NZ):
        for c in range(8):
            send_ref[peer, c * 16 : (c + 1) * 16, :] = key_ref[:, c * 128 : (c + 1) * 128]
        send_ref[peer, 128:144, :] = sums


def middle_kernel(got_ref, send_ref):
    total = jnp.zeros((4, 128), f32)
    for z in range(NZ):
        total = total + join_rows(got_ref[z, 128:144, :])
    sums = split_rows(as_row(total))
    for peer in range(NX):
        for z in range(NZ):
            send_ref[peer, z * 128 : (z + 1) * 128, :] = got_ref[z, 0:128, :]
        send_ref[peer, 1024:1040, :] = sums


def main_kernel(
    factor_ref, x_ref, got_ref, gain_ref, master_ref, gw_ref, plain_ref, slope_ref, send_ref, rows_ref, gx_ref
):
    for x in range(NX):
        for z in range(NZ):
            slot = z * NX + x
            for c in range(8):
                rows_ref[slot * 16 : (slot + 1) * 16, c * 128 : (c + 1) * 128] = got_ref[
                    x, z * 128 + c * 16 : z * 128 + (c + 1) * 16, :
                ]
    total = jnp.zeros((4, 128), f32)
    for x in range(NX):
        total = total + join_rows(got_ref[x, 1024:1040, :])
    inv = lax.rsqrt(as_row(total) * (1.0 / D) + 1e-05)
    col = jnp.broadcast_to(gain_ref[...], (8, F)).T[:, 0:1]
    xt = features_first(x_ref)
    gx = xt * col
    gx_ref[...] = (gx * inv).astype(bf16)
    slope_ref[...] = xt * (inv * inv * inv * (1.0 / D))
    factor = factor_ref[0]
    square = jnp.zeros((1, 256), f32)
    for n in range(4):
        cols = slice(n * 256, (n + 1) * 256)
        part = factor * jnp.dot(gx_ref[...], rows_ref[:, cols], preferred_element_type=f32)
        gw_ref[:, cols] = part
        square = square + jnp.sum(part * part, axis=0, keepdims=True)
    own_sq = jnp.broadcast_to(jnp.sum(square, axis=1, keepdims=True), (1, 128))
    weight = master_ref[...].astype(bf16)
    parts = []
    for n in range(2):
        cols = slice(n * 256, (n + 1) * 256)
        gh = lax.dot_general(
            weight, rows_ref[cols, :], (((1,), (1,)), ((), ())), preferred_element_type=f32
        )
        plain_ref[:, cols] = inv[:, cols] * (col * gh)
        parts.append(jnp.sum(gx[:, cols] * gh, axis=0, keepdims=True))
    packed = jnp.concatenate(parts + [own_sq], axis=1)
    for peer in range(TP):
        send_ref[peer] = packed


def branch_kernel(plain_ref, slope_ref, got_ref, send_ref):
    packed = got_ref[0]
    for peer in range(1, TP):
        packed = packed + got_ref[peer]
    sent = (plain_ref[...] - slope_ref[...] * packed[:, 0:TOK]).astype(bf16)
    layer_sq = split_rows(jnp.concatenate([packed[:, TOK:]] * 4, axis=1))
    for j in range(SEC):
        for q in range(4):
            send_ref[j, q * 16 : (q + 1) * 16, :] = sent[j * 16 : (j + 1) * 16, q * 128 : (q + 1) * 128]
        send_ref[j, 64:72, :] = layer_sq[0:8]


def suffix_kernel(got_ref, back_ref, clip_ref):
    running = jnp.zeros((64, 128), f32)
    norm = jnp.zeros((4, 128), f32)
    for layer in range(SEC - 1, -1, -1):
        s = layer % 2 * 8 + layer // 2
        running = running + got_ref[s, 0:64, :].astype(f32)
        back_ref[s] = running.astype(bf16)
        norm = norm + join_rows(got_ref[s, 64:72, :])
    clip = jnp.minimum(1.0, clip_norm / (jnp.sqrt(norm) + 1e-06))
    clip_ref[...] = jnp.concatenate([clip, clip], axis=0)


def last_kernel(back_ref, out_ref):
    rows = []
    for j in range(SEC):
        rows.append(jnp.concatenate([back_ref[j, q * 16 : (q + 1) * 16, :] for q in range(4)], axis=1))
    out = jnp.concatenate(rows, axis=0).astype(f32).T.reshape(TP, 2, 8, F)
    for m in range(2):
        out_ref[m] = out[:, m].reshape(256, F).astype(bf16)


def on_device(hidden, gain, key_grad, master, moment, second, overflow):
    flag = overflow[0]
    factor = jnp.where(flag == 0, 1.0, jnp.where(flag == 1, 0.5, 0.0)).astype(f32)
    keep = jnp.where(flag == 2, 0.0, 1.0).astype(f32)

    send = call(first_kernel, sds((NZ, 144, 128), bf16), 2, 3 * F * TOK, F * TOK * 2)(
        hidden[0], key_grad.reshape(16, K)
    )
    got = swap(send, "z")
    send = call(middle_kernel, sds((NX, 1040, 128), bf16), 1, 0, 1024 * 1024)(got)
    got = swap(send, "x")
    gw, plain, slope, send = call(
        main_kernel,
        (sds((F, K)), sds((F, TOK)), sds((F, TOK)), sds((TP, 1, TOK + 128))),
        4,
        4 * F * TOK * K,
        4 * 1024 * 1024,
        [pltpu.VMEM((TOK, K), bf16), pltpu.VMEM((F, TOK), bf16)],
        1,
    )(factor[None], hidden[0], got, gain, master[0])
    got = swap(send, ("z", "x"))
    send = call(branch_kernel, sds((SEC, 72, 128), bf16), 3, 3 * F * TOK, 1024 * 1024)(plain, slope, got)
    got = swap(send, ("core", "y"))
    back, clip = call(
        suffix_kernel, (sds((SEC, 64, 128), bf16), sds((8, 128))), 1, 4 * F * TOK, 1024 * 1024
    )(got)
    back = swap(back, ("core", "y"))
    clipped = clip[0, 0] * gw
    moment_new = beta_one * moment[0] + (1.0 - beta_one) * clipped
    second_new = beta_two * second[0] + (1.0 - beta_two) * clipped * clipped
    bias_one = 1.0 - beta_one**step_count
    bias_two = 1.0 - beta_two**step_count
    update = moment_new / bias_one / (jnp.sqrt(second_new / bias_two) + 1e-08) + decay * master[0]
    grad_input = call(last_kernel, sds((2, 256, F), bf16), 1, F * TOK, 1024 * 1024)(back)
    return (grad_input[None], (keep * update)[None])


def solution(mesh):
    fine = Mesh(mesh.devices.reshape(8, 2, NZ, NX), ("y", "core", "z", "x"))
    sec, tp = ("y", "core"), ("z", "x")
    return jax.shard_map(
        on_device,
        mesh=fine,
        in_specs=(
            P(sec, None, None, tp),
            P(sec, tp),
            P(sec, None, tp, None),
            P(sec, tp, None),
            P(sec, tp, None),
            P(sec, tp, None),
            P(sec),
        ),
        out_specs=(P(sec, None, None, tp), P(sec, tp, None)),
        check_vma=False,
    )
```

```python
import jax
import jax.numpy as jnp
from jax import lax
from jax.experimental import pallas as pl
from jax.experimental.pallas import tpu as pltpu
from jax.sharding import Mesh, PartitionSpec as P

D = 8192
SEC, NZ, NX = 16, 8, 4
TP = NZ * NX
TOK = 512
F = 256
K = 1024
f32, bf16 = jnp.float32, jnp.bfloat16

beta_one = 0.9
beta_two = 0.999
decay = 0.1
clip_norm = 1.0
step_count = 10

VM = pl.BlockSpec(memory_space=pltpu.VMEM)
SM = pl.BlockSpec(memory_space=pltpu.SMEM)


def call(body, out_shape, n_in, flops=0, data=0, scratch=(), scalars=0):
    outs = (VM,) * len(out_shape) if isinstance(out_shape, tuple) else VM
    return pl.pallas_call(
        body,
        out_shape=out_shape,
        in_specs=[SM] * scalars + [VM] * n_in,
        out_specs=outs,
        scratch_shapes=list(scratch),
        compiler_params=pltpu.CompilerParams(vmem_limit_bytes=32 * 1024 * 1024),
        cost_estimate=pl.CostEstimate(flops=flops, bytes_accessed=data, transcendentals=0),
    )


def sds(shape, dtype=f32):
    return jax.ShapeDtypeStruct(shape, dtype)


RING = [3 * r % 8 for r in range(8)]
Y_PEERS = [y * 2 + core for core in range(2) for y in RING]
Z_X_PEERS = [z * NX + x for x in range(NX) for z in RING]


def swap(blocks, axis, peers=None):
    groups = None if peers is None else [peers]
    return lax.all_to_all(blocks, axis, split_axis=0, concat_axis=0, tiled=True, axis_index_groups=groups)


def split_rows(row):
    rows = jnp.concatenate([row[:, i * 128 : (i + 1) * 128] for i in range(4)], axis=0)
    high = rows.astype(bf16).astype(f32)
    low = rows - high
    return jnp.concatenate([high, low, jnp.zeros((8, 128), f32)], axis=0).astype(bf16)


def join_rows(rows):
    rows = rows.astype(f32)
    return rows[0:4] + rows[4:8]


def as_row(rows):
    return jnp.concatenate([rows[i : i + 1] for i in range(4)], axis=1)


def features_first(x_ref):
    x = x_ref[...].astype(f32).reshape(2, TP, 8, F)
    return jnp.concatenate([x[0][:, None], x[1][:, None]], axis=1).reshape(TOK, F).T


def first_kernel(x_ref, key_ref, send_ref):
    xt = features_first(x_ref)
    sums = split_rows(jnp.sum(xt * xt, axis=0, keepdims=True))
    for peer in range(NZ):
        for c in range(8):
            send_ref[peer, c * 16 : (c + 1) * 16, :] = key_ref[:, c * 128 : (c + 1) * 128]
        send_ref[peer, 128:144, :] = sums


def middle_kernel(got_ref, send_ref):
    total = jnp.zeros((4, 128), f32)
    for z in range(NZ):
        total = total + join_rows(got_ref[z, 128:144, :])
    sums = split_rows(as_row(total))
    for peer in range(NX):
        for r, z in enumerate(RING):
            send_ref[peer, z * 128 : (z + 1) * 128, :] = got_ref[r, 0:128, :]
        send_ref[peer, 1024:1040, :] = sums


def main_kernel(
    factor_ref, x_ref, got_ref, gain_ref, master_ref, gw_ref, plain_ref, slope_ref, send_ref, rows_ref, gx_ref
):
    for x in range(NX):
        for z in range(NZ):
            slot = z * NX + x
            for c in range(8):
                rows_ref[slot * 16 : (slot + 1) * 16, c * 128 : (c + 1) * 128] = got_ref[
                    x, z * 128 + c * 16 : z * 128 + (c + 1) * 16, :
                ]
    total = jnp.zeros((4, 128), f32)
    for x in range(NX):
        total = total + join_rows(got_ref[x, 1024:1040, :])
    inv = lax.rsqrt(as_row(total) * (1.0 / D) + 1e-05)
    col = jnp.broadcast_to(gain_ref[...], (8, F)).T[:, 0:1]
    xt = features_first(x_ref)
    gx = xt * col
    gx_ref[...] = (gx * inv).astype(bf16)
    slope_ref[...] = xt * (inv * inv * inv * (1.0 / D))
    factor = factor_ref[0]
    square = jnp.zeros((1, 256), f32)
    for n in range(4):
        cols = slice(n * 256, (n + 1) * 256)
        part = factor * jnp.dot(gx_ref[...], rows_ref[:, cols], preferred_element_type=f32)
        gw_ref[:, cols] = part
        square = square + jnp.sum(part * part, axis=0, keepdims=True)
    own_sq = jnp.broadcast_to(jnp.sum(square, axis=1, keepdims=True), (1, 128))
    weight = master_ref[...].astype(bf16)
    parts = []
    for n in range(2):
        cols = slice(n * 256, (n + 1) * 256)
        gh = lax.dot_general(
            weight, rows_ref[cols, :], (((1,), (1,)), ((), ())), preferred_element_type=f32
        )
        plain_ref[:, cols] = inv[:, cols] * (col * gh)
        parts.append(jnp.sum(gx[:, cols] * gh, axis=0, keepdims=True))
    packed = jnp.concatenate(parts + [own_sq], axis=1)
    for peer in range(TP):
        send_ref[peer] = packed


def branch_kernel(plain_ref, slope_ref, got_ref, send_ref):
    packed = got_ref[0]
    for peer in range(1, TP):
        packed = packed + got_ref[peer]
    sent = (plain_ref[...] - slope_ref[...] * packed[:, 0:TOK]).astype(bf16)
    layer_sq = split_rows(jnp.concatenate([packed[:, TOK:]] * 4, axis=1))
    for j in range(SEC):
        for q in range(4):
            send_ref[j, q * 16 : (q + 1) * 16, :] = sent[j * 16 : (j + 1) * 16, q * 128 : (q + 1) * 128]
        send_ref[j, 64:72, :] = layer_sq[0:8]


def suffix_kernel(got_ref, back_ref, clip_ref):
    running = jnp.zeros((64, 128), f32)
    norm = jnp.zeros((4, 128), f32)
    for layer in range(SEC - 1, -1, -1):
        s = Y_PEERS.index(layer)
        running = running + got_ref[s, 0:64, :].astype(f32)
        back_ref[s] = running.astype(bf16)
        norm = norm + join_rows(got_ref[s, 64:72, :])
    clip = jnp.minimum(1.0, clip_norm / (jnp.sqrt(norm) + 1e-06))
    clip_ref[...] = jnp.concatenate([clip, clip], axis=0)


def last_kernel(back_ref, out_ref):
    rows = []
    for j in range(SEC):
        rows.append(jnp.concatenate([back_ref[j, q * 16 : (q + 1) * 16, :] for q in range(4)], axis=1))
    out = jnp.concatenate(rows, axis=0).astype(f32).T.reshape(TP, 2, 8, F)
    for m in range(2):
        out_ref[m] = out[:, m].reshape(256, F).astype(bf16)


def on_device(hidden, gain, key_grad, master, moment, second, overflow):
    flag = overflow[0]
    factor = jnp.where(flag == 0, 1.0, jnp.where(flag == 1, 0.5, 0.0)).astype(f32)
    keep = jnp.where(flag == 2, 0.0, 1.0).astype(f32)

    send = call(first_kernel, sds((NZ, 144, 128), bf16), 2, 3 * F * TOK, F * TOK * 2)(
        hidden[0], key_grad.reshape(16, K)
    )
    got = swap(send, "z", RING)
    send = call(middle_kernel, sds((NX, 1040, 128), bf16), 1, 0, 1024 * 1024)(got)
    got = swap(send, "x")
    gw, plain, slope, send = call(
        main_kernel,
        (sds((F, K)), sds((F, TOK)), sds((F, TOK)), sds((TP, 1, TOK + 128))),
        4,
        4 * F * TOK * K,
        4 * 1024 * 1024,
        [pltpu.VMEM((TOK, K), bf16), pltpu.VMEM((F, TOK), bf16)],
        1,
    )(factor[None], hidden[0], got, gain, master[0])
    got = swap(send, ("z", "x"), Z_X_PEERS)
    send = call(branch_kernel, sds((SEC, 72, 128), bf16), 3, 3 * F * TOK, 1024 * 1024)(plain, slope, got)
    got = swap(send, ("y", "core"), Y_PEERS)
    back, clip = call(
        suffix_kernel, (sds((SEC, 64, 128), bf16), sds((8, 128))), 1, 4 * F * TOK, 1024 * 1024
    )(got)
    back = swap(back, ("y", "core"), Y_PEERS)
    clipped = clip[0, 0] * gw
    moment_new = beta_one * moment[0] + (1.0 - beta_one) * clipped
    second_new = beta_two * second[0] + (1.0 - beta_two) * clipped * clipped
    bias_one = 1.0 - beta_one**step_count
    bias_two = 1.0 - beta_two**step_count
    update = moment_new / bias_one / (jnp.sqrt(second_new / bias_two) + 1e-08) + decay * master[0]
    grad_input = call(last_kernel, sds((2, 256, F), bf16), 1, F * TOK, 1024 * 1024)(back)
    return (grad_input[None], (keep * update)[None])


def solution(mesh):
    fine = Mesh(mesh.devices.reshape(8, 2, NZ, NX), ("y", "core", "z", "x"))
    sec, tp = ("y", "core"), ("z", "x")
    return jax.shard_map(
        on_device,
        mesh=fine,
        in_specs=(
            P(sec, None, None, tp),
            P(sec, tp),
            P(sec, None, tp, None),
            P(sec, tp, None),
            P(sec, tp, None),
            P(sec, tp, None),
            P(sec),
        ),
        out_specs=(P(sec, None, None, tp), P(sec, tp, None)),
        check_vma=False,
    )
```

```python
import jax
import jax.numpy as jnp
from jax import lax
from jax.experimental import pallas as pl
from jax.experimental.pallas import tpu as pltpu
from jax.sharding import Mesh, PartitionSpec as P

D = 8192
SEC, NZ, NX = 16, 8, 4
TP = NZ * NX
TOK = 512
F = 256
K = 1024
f32, bf16 = jnp.float32, jnp.bfloat16

beta_one = 0.9
beta_two = 0.999
decay = 0.1
clip_norm = 1.0
step_count = 10

VM = pl.BlockSpec(memory_space=pltpu.VMEM)
SM = pl.BlockSpec(memory_space=pltpu.SMEM)


def call(body, out_shape, n_in, flops=0, data=0, scratch=(), scalars=0):
    outs = (VM,) * len(out_shape) if isinstance(out_shape, tuple) else VM
    return pl.pallas_call(
        body,
        out_shape=out_shape,
        in_specs=[SM] * scalars + [VM] * n_in,
        out_specs=outs,
        scratch_shapes=list(scratch),
        compiler_params=pltpu.CompilerParams(vmem_limit_bytes=32 * 1024 * 1024),
        cost_estimate=pl.CostEstimate(flops=flops, bytes_accessed=data, transcendentals=0),
    )


def sds(shape, dtype=f32):
    return jax.ShapeDtypeStruct(shape, dtype)


RING = [3 * r % 8 for r in range(8)]
Y_PEERS = [y * 2 + core for core in range(2) for y in RING]


def swap(blocks, axis, peers=None):
    groups = None if peers is None else [peers]
    return lax.all_to_all(blocks, axis, split_axis=0, concat_axis=0, tiled=True, axis_index_groups=groups)


def split_rows(row):
    rows = jnp.concatenate([row[:, i * 128 : (i + 1) * 128] for i in range(4)], axis=0)
    high = rows.astype(bf16).astype(f32)
    low = rows - high
    return jnp.concatenate([high, low, jnp.zeros((8, 128), f32)], axis=0).astype(bf16)


def join_rows(rows):
    rows = rows.astype(f32)
    return rows[0:4] + rows[4:8]


def as_row(rows):
    return jnp.concatenate([rows[i : i + 1] for i in range(4)], axis=1)


def features_first(x_ref):
    x = x_ref[...].astype(f32).reshape(2, TP, 8, F)
    return jnp.concatenate([x[0][:, None], x[1][:, None]], axis=1).reshape(TOK, F).T


def first_kernel(x_ref, key_ref, send_ref):
    xt = features_first(x_ref)
    sums = split_rows(jnp.sum(xt * xt, axis=0, keepdims=True))
    for peer in range(NZ):
        for c in range(8):
            send_ref[peer, c * 16 : (c + 1) * 16, :] = key_ref[:, c * 128 : (c + 1) * 128]
        send_ref[peer, 128:136, :] = sums[0:8]


def middle_kernel(got_ref, send_ref):
    total = jnp.zeros((4, 128), f32)
    for z in range(NZ):
        total = total + join_rows(got_ref[z, 128:136, :])
    sums = split_rows(as_row(total))
    for peer in range(NX):
        for r, z in enumerate(RING):
            send_ref[peer, z * 128 : (z + 1) * 128, :] = got_ref[r, 0:128, :]
        send_ref[peer, 1024:1032, :] = sums[0:8]


def main_kernel(
    factor_ref, x_ref, got_ref, gain_ref, master_ref, gw_ref, plain_ref, slope_ref, send_ref, rows_ref, gx_ref
):
    for x in range(NX):
        for z in range(NZ):
            slot = z * NX + x
            for c in range(8):
                rows_ref[slot * 16 : (slot + 1) * 16, c * 128 : (c + 1) * 128] = got_ref[
                    x, z * 128 + c * 16 : z * 128 + (c + 1) * 16, :
                ]
    total = jnp.zeros((4, 128), f32)
    for x in range(NX):
        total = total + join_rows(got_ref[x, 1024:1032, :])
    inv = lax.rsqrt(as_row(total) * (1.0 / D) + 1e-05)
    col = jnp.broadcast_to(gain_ref[...], (8, F)).T[:, 0:1]
    xt = features_first(x_ref)
    gx = xt * col
    gx_ref[...] = (gx * inv).astype(bf16)
    slope_ref[...] = xt * (inv * inv * inv * (1.0 / D))
    factor = factor_ref[0]
    square = jnp.zeros((1, 256), f32)
    for n in range(4):
        cols = slice(n * 256, (n + 1) * 256)
        part = factor * jnp.dot(gx_ref[...], rows_ref[:, cols], preferred_element_type=f32)
        gw_ref[:, cols] = part
        square = square + jnp.sum(part * part, axis=0, keepdims=True)
    own_sq = jnp.broadcast_to(jnp.sum(square, axis=1, keepdims=True), (1, 128))
    weight = master_ref[...].astype(bf16)
    parts = []
    for n in range(2):
        cols = slice(n * 256, (n + 1) * 256)
        gh = lax.dot_general(
            weight, rows_ref[cols, :], (((1,), (1,)), ((), ())), preferred_element_type=f32
        )
        plain_ref[:, cols] = inv[:, cols] * (col * gh)
        parts.append(jnp.sum(gx[:, cols] * gh, axis=0, keepdims=True))
    packed = jnp.concatenate(parts + [own_sq], axis=1)
    for peer in range(TP):
        send_ref[peer] = packed


def branch_kernel(plain_ref, slope_ref, got_ref, send_ref):
    packed = got_ref[0]
    for peer in range(1, TP):
        packed = packed + got_ref[peer]
    sent = (plain_ref[...] - slope_ref[...] * packed[:, 0:TOK]).astype(bf16)
    layer_sq = split_rows(jnp.concatenate([packed[:, TOK:]] * 4, axis=1))
    for j in range(SEC):
        for q in range(4):
            send_ref[j, q * 16 : (q + 1) * 16, :] = sent[j * 16 : (j + 1) * 16, q * 128 : (q + 1) * 128]
        send_ref[j, 64:72, :] = layer_sq[0:8]


def suffix_kernel(got_ref, back_ref, clip_ref):
    running = jnp.zeros((64, 128), f32)
    norm = jnp.zeros((4, 128), f32)
    for layer in range(SEC - 1, -1, -1):
        s = Y_PEERS.index(layer)
        running = running + got_ref[s, 0:64, :].astype(f32)
        back_ref[s] = running.astype(bf16)
        norm = norm + join_rows(got_ref[s, 64:72, :])
    clip = jnp.minimum(1.0, clip_norm / (jnp.sqrt(norm) + 1e-06))
    clip_ref[...] = jnp.concatenate([clip, clip], axis=0)


def last_kernel(back_ref, out_ref):
    rows = []
    for j in range(SEC):
        rows.append(jnp.concatenate([back_ref[j, q * 16 : (q + 1) * 16, :] for q in range(4)], axis=1))
    out = jnp.concatenate(rows, axis=0).astype(f32).T.reshape(TP, 2, 8, F)
    for m in range(2):
        out_ref[m] = out[:, m].reshape(256, F).astype(bf16)


def on_device(hidden, gain, key_grad, master, moment, second, overflow):
    flag = overflow[0]
    factor = jnp.where(flag == 0, 1.0, jnp.where(flag == 1, 0.5, 0.0)).astype(f32)
    keep = jnp.where(flag == 2, 0.0, 1.0).astype(f32)

    send = call(first_kernel, sds((NZ, 136, 128), bf16), 2, 3 * F * TOK, F * TOK * 2)(
        hidden[0], key_grad.reshape(16, K)
    )
    got = swap(send, "z", RING)
    send = call(middle_kernel, sds((NX, 1032, 128), bf16), 1, 0, 1024 * 1024)(got)
    got = swap(send, "x")
    gw, plain, slope, send = call(
        main_kernel,
        (sds((F, K)), sds((F, TOK)), sds((F, TOK)), sds((TP, 1, TOK + 128))),
        4,
        4 * F * TOK * K,
        4 * 1024 * 1024,
        [pltpu.VMEM((TOK, K), bf16), pltpu.VMEM((F, TOK), bf16)],
        1,
    )(factor[None], hidden[0], got, gain, master[0])
    got = swap(send, ("z", "x"))
    send = call(branch_kernel, sds((SEC, 72, 128), bf16), 3, 3 * F * TOK, 1024 * 1024)(plain, slope, got)
    got = swap(send, ("y", "core"), Y_PEERS)
    back, clip = call(
        suffix_kernel, (sds((SEC, 64, 128), bf16), sds((8, 128))), 1, 4 * F * TOK, 1024 * 1024
    )(got)
    back = swap(back, ("y", "core"), Y_PEERS)
    clipped = clip[0, 0] * gw
    moment_new = beta_one * moment[0] + (1.0 - beta_one) * clipped
    second_new = beta_two * second[0] + (1.0 - beta_two) * clipped * clipped
    bias_one = 1.0 - beta_one**step_count
    bias_two = 1.0 - beta_two**step_count
    update = moment_new / bias_one / (jnp.sqrt(second_new / bias_two) + 1e-08) + decay * master[0]
    grad_input = call(last_kernel, sds((2, 256, F), bf16), 1, F * TOK, 1024 * 1024)(back)
    return (grad_input[None], (keep * update)[None])


def solution(mesh):
    fine = Mesh(mesh.devices.reshape(8, 2, NZ, NX), ("y", "core", "z", "x"))
    sec, tp = ("y", "core"), ("z", "x")
    return jax.shard_map(
        on_device,
        mesh=fine,
        in_specs=(
            P(sec, None, None, tp),
            P(sec, tp),
            P(sec, None, tp, None),
            P(sec, tp, None),
            P(sec, tp, None),
            P(sec, tp, None),
            P(sec),
        ),
        out_specs=(P(sec, None, None, tp), P(sec, tp, None)),
        check_vma=False,
    )
```

```python
import jax
import jax.numpy as jnp
from jax import lax
from jax.experimental import pallas as pl
from jax.experimental.pallas import tpu as pltpu
from jax.sharding import Mesh, PartitionSpec as P

D = 8192
SEC, NZ, NX = 16, 8, 4
TP = NZ * NX
TOK = 512
F = 256
K = 1024
f32, bf16 = jnp.float32, jnp.bfloat16

beta_one = 0.9
beta_two = 0.999
decay = 0.1
clip_norm = 1.0
step_count = 10

VM = pl.BlockSpec(memory_space=pltpu.VMEM)
SM = pl.BlockSpec(memory_space=pltpu.SMEM)


def call(body, out_shape, n_in, flops=0, data=0, scratch=(), scalars=0):
    outs = (VM,) * len(out_shape) if isinstance(out_shape, tuple) else VM
    return pl.pallas_call(
        body,
        out_shape=out_shape,
        in_specs=[SM] * scalars + [VM] * n_in,
        out_specs=outs,
        scratch_shapes=list(scratch),
        compiler_params=pltpu.CompilerParams(vmem_limit_bytes=32 * 1024 * 1024),
        cost_estimate=pl.CostEstimate(flops=flops, bytes_accessed=data, transcendentals=0),
    )


def sds(shape, dtype=f32):
    return jax.ShapeDtypeStruct(shape, dtype)


RING = [3 * r % 8 for r in range(8)]
Y_PEERS = [y * 2 + core for core in range(2) for y in RING]


def swap(blocks, axis, peers=None):
    groups = None if peers is None else [peers]
    return lax.all_to_all(blocks, axis, split_axis=0, concat_axis=0, tiled=True, axis_index_groups=groups)


def split_rows(row):
    rows = jnp.concatenate([row[:, i * 128 : (i + 1) * 128] for i in range(4)], axis=0)
    high = rows.astype(bf16).astype(f32)
    low = rows - high
    return jnp.concatenate([high, low, jnp.zeros((8, 128), f32)], axis=0).astype(bf16)


def join_rows(rows):
    rows = rows.astype(f32)
    return rows[0:4] + rows[4:8]


def as_row(rows):
    return jnp.concatenate([rows[i : i + 1] for i in range(4)], axis=1)


def features_first(x_ref):
    x = x_ref[...].astype(f32).reshape(2, TP, 8, F)
    return jnp.concatenate([x[0][:, None], x[1][:, None]], axis=1).reshape(TOK, F).T


def key_kernel(key_ref, block_ref):
    for c in range(8):
        block_ref[c * 16 : (c + 1) * 16, :] = key_ref[:, c * 128 : (c + 1) * 128]


def first_kernel(flag_ref, x_ref, block_ref, send_ref, flags_ref):
    xt = features_first(x_ref)
    sums = split_rows(jnp.sum(xt * xt, axis=0, keepdims=True))
    for peer in range(NZ):
        send_ref[peer, 0:128, :] = block_ref[...]
        send_ref[peer, 128:136, :] = sums[0:8]
    flag = flag_ref[0]
    factor = jnp.where(flag == 0, 1.0, jnp.where(flag == 1, 0.5, 0.0)).astype(f32)
    keep = jnp.where(flag == 2, 0.0, 1.0).astype(f32)
    flags_ref[...] = jnp.concatenate([jnp.full((4, 128), factor), jnp.full((4, 128), keep)], axis=0)


def middle_kernel(got_ref, send_ref):
    total = jnp.zeros((4, 128), f32)
    for z in range(NZ):
        total = total + join_rows(got_ref[z, 128:136, :])
    sums = split_rows(as_row(total))
    for peer in range(NX):
        for r, z in enumerate(RING):
            send_ref[peer, z * 128 : (z + 1) * 128, :] = got_ref[r, 0:128, :]
        send_ref[peer, 1024:1032, :] = sums[0:8]


def main_kernel(
    flags_ref, x_ref, got_ref, gain_ref, master_ref, gw_ref, plain_ref, slope_ref, send_ref, rows_ref, gx_ref
):
    for x in range(NX):
        for z in range(NZ):
            slot = z * NX + x
            for c in range(8):
                rows_ref[slot * 16 : (slot + 1) * 16, c * 128 : (c + 1) * 128] = got_ref[
                    x, z * 128 + c * 16 : z * 128 + (c + 1) * 16, :
                ]
    total = jnp.zeros((4, 128), f32)
    for x in range(NX):
        total = total + join_rows(got_ref[x, 1024:1032, :])
    inv = lax.rsqrt(as_row(total) * (1.0 / D) + 1e-05)
    col = jnp.broadcast_to(gain_ref[...], (8, F)).T[:, 0:1]
    xt = features_first(x_ref)
    gx = xt * col
    gx_ref[...] = (gx * inv).astype(bf16)
    slope_ref[...] = xt * (inv * inv * inv * (1.0 / D))
    factor = flags_ref[0:1, 0:1]
    square = jnp.zeros((1, 256), f32)
    for n in range(4):
        cols = slice(n * 256, (n + 1) * 256)
        part = factor * jnp.dot(gx_ref[...], rows_ref[:, cols], preferred_element_type=f32)
        gw_ref[:, cols] = part
        square = square + jnp.sum(part * part, axis=0, keepdims=True)
    own_sq = jnp.broadcast_to(jnp.sum(square, axis=1, keepdims=True), (1, 128))
    weight = master_ref[...].astype(bf16)
    parts = []
    for n in range(2):
        cols = slice(n * 256, (n + 1) * 256)
        gh = lax.dot_general(
            weight, rows_ref[cols, :], (((1,), (1,)), ((), ())), preferred_element_type=f32
        )
        plain_ref[:, cols] = inv[:, cols] * (col * gh)
        parts.append(jnp.sum(gx[:, cols] * gh, axis=0, keepdims=True))
    packed = jnp.concatenate(parts + [own_sq], axis=1)
    for peer in range(TP):
        send_ref[peer] = packed


def branch_kernel(plain_ref, slope_ref, got_ref, send_ref):
    packed = got_ref[0]
    for peer in range(1, TP):
        packed = packed + got_ref[peer]
    sent = (plain_ref[...] - slope_ref[...] * packed[:, 0:TOK]).astype(bf16)
    layer_sq = split_rows(jnp.concatenate([packed[:, TOK:]] * 4, axis=1))
    for j in range(SEC):
        for q in range(4):
            send_ref[j, q * 16 : (q + 1) * 16, :] = sent[j * 16 : (j + 1) * 16, q * 128 : (q + 1) * 128]
        send_ref[j, 64:72, :] = layer_sq[0:8]


def suffix_kernel(got_ref, flags_ref, back_ref, clip_ref):
    running = jnp.zeros((64, 128), f32)
    norm = jnp.zeros((4, 128), f32)
    for layer in range(SEC - 1, -1, -1):
        s = Y_PEERS.index(layer)
        running = running + got_ref[s, 0:64, :].astype(f32)
        back_ref[s] = running.astype(bf16)
        norm = norm + join_rows(got_ref[s, 64:72, :])
    clip = jnp.minimum(1.0, clip_norm / (jnp.sqrt(norm) + 1e-06))
    clip_ref[...] = jnp.concatenate([clip, flags_ref[4:8, :]], axis=0)


def last_kernel(back_ref, out_ref):
    rows = []
    for j in range(SEC):
        rows.append(jnp.concatenate([back_ref[j, q * 16 : (q + 1) * 16, :] for q in range(4)], axis=1))
    out = jnp.concatenate(rows, axis=0).astype(f32).T.reshape(TP, 2, 8, F)
    for m in range(2):
        out_ref[m] = out[:, m].reshape(256, F).astype(bf16)


def on_device(hidden, gain, key_grad, master, moment, second, overflow):
    block = call(key_kernel, sds((128, 128), bf16), 1, 0, 64 * 1024)(key_grad.reshape(16, K))
    send, flags = call(
        first_kernel, (sds((NZ, 136, 128), bf16), sds((8, 128))), 2, 3 * F * TOK, F * TOK * 2, (), 1
    )(overflow, hidden[0], block)
    got = swap(send, "z", RING)
    send = call(middle_kernel, sds((NX, 1032, 128), bf16), 1, 0, 1024 * 1024)(got)
    got = swap(send, "x")
    gw, plain, slope, send = call(
        main_kernel,
        (sds((F, K)), sds((F, TOK)), sds((F, TOK)), sds((TP, 1, TOK + 128))),
        5,
        4 * F * TOK * K,
        4 * 1024 * 1024,
        [pltpu.VMEM((TOK, K), bf16), pltpu.VMEM((F, TOK), bf16)],
    )(flags, hidden[0], got, gain, master[0])
    got = swap(send, ("z", "x"))
    send = call(branch_kernel, sds((SEC, 72, 128), bf16), 3, 3 * F * TOK, 1024 * 1024)(plain, slope, got)
    got = swap(send, ("y", "core"), Y_PEERS)
    back, clip = call(
        suffix_kernel, (sds((SEC, 64, 128), bf16), sds((8, 128))), 2, 4 * F * TOK, 1024 * 1024
    )(got, flags)
    back = swap(back, ("y", "core"), Y_PEERS)
    clipped = clip[0, 0] * gw
    moment_new = beta_one * moment[0] + (1.0 - beta_one) * clipped
    second_new = beta_two * second[0] + (1.0 - beta_two) * clipped * clipped
    bias_one = 1.0 - beta_one**step_count
    bias_two = 1.0 - beta_two**step_count
    update = moment_new / bias_one / (jnp.sqrt(second_new / bias_two) + 1e-08) + decay * master[0]
    grad_input = call(last_kernel, sds((2, 256, F), bf16), 1, F * TOK, 1024 * 1024)(back)
    return (grad_input[None], (clip[4, 0] * update)[None])


def solution(mesh):
    fine = Mesh(mesh.devices.reshape(8, 2, NZ, NX), ("y", "core", "z", "x"))
    sec, tp = ("y", "core"), ("z", "x")
    return jax.shard_map(
        on_device,
        mesh=fine,
        in_specs=(
            P(sec, None, None, tp),
            P(sec, tp),
            P(sec, None, tp, None),
            P(sec, tp, None),
            P(sec, tp, None),
            P(sec, tp, None),
            P(sec),
        ),
        out_specs=(P(sec, None, None, tp), P(sec, tp, None)),
        check_vma=False,
    )
```

```python
import jax
import jax.numpy as jnp
from jax import lax
from jax.experimental import pallas as pl
from jax.experimental.pallas import tpu as pltpu
from jax.sharding import Mesh, PartitionSpec as P

D = 8192
SEC, NZ, NX = 16, 8, 4
TP = NZ * NX
TOK = 512
F = 256
K = 1024
f32, bf16 = jnp.float32, jnp.bfloat16

beta_one = 0.9
beta_two = 0.999
decay = 0.1
clip_norm = 1.0
step_count = 10

VM = pl.BlockSpec(memory_space=pltpu.VMEM)
SM = pl.BlockSpec(memory_space=pltpu.SMEM)


def call(body, out_shape, n_in, flops=0, data=0, scratch=(), scalars=0):
    outs = (VM,) * len(out_shape) if isinstance(out_shape, tuple) else VM
    return pl.pallas_call(
        body,
        out_shape=out_shape,
        in_specs=[SM] * scalars + [VM] * n_in,
        out_specs=outs,
        scratch_shapes=list(scratch),
        compiler_params=pltpu.CompilerParams(vmem_limit_bytes=32 * 1024 * 1024),
        cost_estimate=pl.CostEstimate(flops=flops, bytes_accessed=data, transcendentals=0),
    )


def sds(shape, dtype=f32):
    return jax.ShapeDtypeStruct(shape, dtype)


RING = [0, 1, 7, 2, 6, 3, 5, 4]
X_RING = [0, 1, 3, 2]
Y_PEERS = [y * 2 + core for core in range(2) for y in RING]


def swap(blocks, axis, peers=None):
    groups = None if peers is None else [peers]
    return lax.all_to_all(blocks, axis, split_axis=0, concat_axis=0, tiled=True, axis_index_groups=groups)


def split_rows(row):
    rows = jnp.concatenate([row[:, i * 128 : (i + 1) * 128] for i in range(4)], axis=0)
    high = rows.astype(bf16).astype(f32)
    low = rows - high
    return jnp.concatenate([high, low, jnp.zeros((8, 128), f32)], axis=0).astype(bf16)


def join_rows(rows):
    rows = rows.astype(f32)
    return rows[0:4] + rows[4:8]


def as_row(rows):
    return jnp.concatenate([rows[i : i + 1] for i in range(4)], axis=1)


def features_first(x_ref):
    x = x_ref[...].astype(f32).reshape(2, TP, 8, F)
    return jnp.concatenate([x[0][:, None], x[1][:, None]], axis=1).reshape(TOK, F).T


def key_kernel(key_ref, block_ref):
    for c in range(8):
        block_ref[c * 16 : (c + 1) * 16, :] = key_ref[:, c * 128 : (c + 1) * 128]


def first_kernel(flag_ref, x_ref, block_ref, send_ref, flags_ref):
    xt = features_first(x_ref)
    sums = split_rows(jnp.sum(xt * xt, axis=0, keepdims=True))
    for peer in range(NZ):
        send_ref[peer, 0:128, :] = block_ref[...]
        send_ref[peer, 128:136, :] = sums[0:8]
    flag = flag_ref[0]
    factor = jnp.where(flag == 0, 1.0, jnp.where(flag == 1, 0.5, 0.0)).astype(f32)
    keep = jnp.where(flag == 2, 0.0, 1.0).astype(f32)
    flags_ref[...] = jnp.concatenate([jnp.full((4, 128), factor), jnp.full((4, 128), keep)], axis=0)


def middle_kernel(got_ref, send_ref):
    total = jnp.zeros((4, 128), f32)
    for z in range(NZ):
        total = total + join_rows(got_ref[z, 128:136, :])
    sums = split_rows(as_row(total))
    for peer in range(NX):
        for r, z in enumerate(RING):
            send_ref[peer, z * 128 : (z + 1) * 128, :] = got_ref[r, 0:128, :]
        send_ref[peer, 1024:1032, :] = sums[0:8]


def main_kernel(
    flags_ref, x_ref, got_ref, gain_ref, master_ref, gw_ref, plain_ref, slope_ref, send_ref, rows_ref, gx_ref
):
    for r, x in enumerate(X_RING):
        for z in range(NZ):
            slot = z * NX + x
            for c in range(8):
                rows_ref[slot * 16 : (slot + 1) * 16, c * 128 : (c + 1) * 128] = got_ref[
                    r, z * 128 + c * 16 : z * 128 + (c + 1) * 16, :
                ]
    total = jnp.zeros((4, 128), f32)
    for x in range(NX):
        total = total + join_rows(got_ref[x, 1024:1032, :])
    inv = lax.rsqrt(as_row(total) * (1.0 / D) + 1e-05)
    col = jnp.broadcast_to(gain_ref[...], (8, F)).T[:, 0:1]
    xt = features_first(x_ref)
    gx = xt * col
    gx_ref[...] = (gx * inv).astype(bf16)
    slope_ref[...] = xt * (inv * inv * inv * (1.0 / D))
    factor = flags_ref[0:1, 0:1]
    square = jnp.zeros((1, 256), f32)
    for n in range(4):
        cols = slice(n * 256, (n + 1) * 256)
        part = factor * jnp.dot(gx_ref[...], rows_ref[:, cols], preferred_element_type=f32)
        gw_ref[:, cols] = part
        square = square + jnp.sum(part * part, axis=0, keepdims=True)
    own_sq = jnp.broadcast_to(jnp.sum(square, axis=1, keepdims=True), (1, 128))
    weight = master_ref[...].astype(bf16)
    parts = []
    for n in range(2):
        cols = slice(n * 256, (n + 1) * 256)
        gh = lax.dot_general(
            weight, rows_ref[cols, :], (((1,), (1,)), ((), ())), preferred_element_type=f32
        )
        plain_ref[:, cols] = inv[:, cols] * (col * gh)
        parts.append(jnp.sum(gx[:, cols] * gh, axis=0, keepdims=True))
    packed = jnp.concatenate(parts + [own_sq], axis=1)
    for peer in range(TP):
        send_ref[peer] = packed


def branch_kernel(plain_ref, slope_ref, got_ref, send_ref):
    packed = got_ref[0]
    for peer in range(1, TP):
        packed = packed + got_ref[peer]
    sent = (plain_ref[...] - slope_ref[...] * packed[:, 0:TOK]).astype(bf16)
    layer_sq = split_rows(jnp.concatenate([packed[:, TOK:]] * 4, axis=1))
    for j in range(SEC):
        for q in range(4):
            send_ref[j, q * 16 : (q + 1) * 16, :] = sent[j * 16 : (j + 1) * 16, q * 128 : (q + 1) * 128]
        send_ref[j, 64:72, :] = layer_sq[0:8]


def suffix_kernel(got_ref, flags_ref, back_ref, clip_ref):
    running = jnp.zeros((64, 128), f32)
    norm = jnp.zeros((4, 128), f32)
    for layer in range(SEC - 1, -1, -1):
        s = Y_PEERS.index(layer)
        running = running + got_ref[s, 0:64, :].astype(f32)
        back_ref[s] = running.astype(bf16)
        norm = norm + join_rows(got_ref[s, 64:72, :])
    clip = jnp.minimum(1.0, clip_norm / (jnp.sqrt(norm) + 1e-06))
    clip_ref[...] = jnp.concatenate([clip, flags_ref[4:8, :]], axis=0)


def last_kernel(back_ref, out_ref):
    rows = []
    for j in range(SEC):
        rows.append(jnp.concatenate([back_ref[j, q * 16 : (q + 1) * 16, :] for q in range(4)], axis=1))
    out = jnp.concatenate(rows, axis=0).astype(f32).T.reshape(TP, 2, 8, F)
    for m in range(2):
        out_ref[m] = out[:, m].reshape(256, F).astype(bf16)


def on_device(hidden, gain, key_grad, master, moment, second, overflow):
    block = call(key_kernel, sds((128, 128), bf16), 1, 0, 64 * 1024)(key_grad.reshape(16, K))
    send, flags = call(
        first_kernel, (sds((NZ, 136, 128), bf16), sds((8, 128))), 2, 3 * F * TOK, F * TOK * 2, (), 1
    )(overflow, hidden[0], block)
    got = swap(send, "z", RING)
    send = call(middle_kernel, sds((NX, 1032, 128), bf16), 1, 0, 1024 * 1024)(got)
    got = swap(send, "x", X_RING)
    gw, plain, slope, send = call(
        main_kernel,
        (sds((F, K)), sds((F, TOK)), sds((F, TOK)), sds((TP, 1, TOK + 128))),
        5,
        4 * F * TOK * K,
        4 * 1024 * 1024,
        [pltpu.VMEM((TOK, K), bf16), pltpu.VMEM((F, TOK), bf16)],
    )(flags, hidden[0], got, gain, master[0])
    got = swap(send, ("z", "x"))
    send = call(branch_kernel, sds((SEC, 72, 128), bf16), 3, 3 * F * TOK, 1024 * 1024)(plain, slope, got)
    got = swap(send, ("y", "core"), Y_PEERS)
    back, clip = call(
        suffix_kernel, (sds((SEC, 64, 128), bf16), sds((8, 128))), 2, 4 * F * TOK, 1024 * 1024
    )(got, flags)
    back = swap(back, ("y", "core"), Y_PEERS)
    clipped = clip[0, 0] * gw
    moment_new = beta_one * moment[0] + (1.0 - beta_one) * clipped
    second_new = beta_two * second[0] + (1.0 - beta_two) * clipped * clipped
    bias_one = 1.0 - beta_one**step_count
    bias_two = 1.0 - beta_two**step_count
    update = moment_new / bias_one / (jnp.sqrt(second_new / bias_two) + 1e-08) + decay * master[0]
    grad_input = call(last_kernel, sds((2, 256, F), bf16), 1, F * TOK, 1024 * 1024)(back)
    return (grad_input[None], (clip[4, 0] * update)[None])


def solution(mesh):
    fine = Mesh(mesh.devices.reshape(8, 2, NZ, NX), ("y", "core", "z", "x"))
    sec, tp = ("y", "core"), ("z", "x")
    return jax.shard_map(
        on_device,
        mesh=fine,
        in_specs=(
            P(sec, None, None, tp),
            P(sec, tp),
            P(sec, None, tp, None),
            P(sec, tp, None),
            P(sec, tp, None),
            P(sec, tp, None),
            P(sec),
        ),
        out_specs=(P(sec, None, None, tp), P(sec, tp, None)),
        check_vma=False,
    )
```

```python
import jax
import jax.numpy as jnp
from jax import lax
from jax.experimental import pallas as pl
from jax.experimental.pallas import tpu as pltpu
from jax.sharding import Mesh, PartitionSpec as P

D = 8192
SEC, NZ, NX = 16, 8, 4
TP = NZ * NX
TOK = 512
F = 256
K = 1024
f32, bf16 = jnp.float32, jnp.bfloat16

beta_one = 0.9
beta_two = 0.999
decay = 0.1
clip_norm = 1.0
step_count = 10

VM = pl.BlockSpec(memory_space=pltpu.VMEM)
SM = pl.BlockSpec(memory_space=pltpu.SMEM)


def call(body, out_shape, n_in, flops=0, data=0, scratch=(), scalars=0):
    outs = (VM,) * len(out_shape) if isinstance(out_shape, tuple) else VM
    return pl.pallas_call(
        body,
        out_shape=out_shape,
        in_specs=[SM] * scalars + [VM] * n_in,
        out_specs=outs,
        scratch_shapes=list(scratch),
        compiler_params=pltpu.CompilerParams(vmem_limit_bytes=32 * 1024 * 1024),
        cost_estimate=pl.CostEstimate(flops=flops, bytes_accessed=data, transcendentals=0),
    )


def sds(shape, dtype=f32):
    return jax.ShapeDtypeStruct(shape, dtype)


RING = [3 * r % 8 for r in range(8)]
MIXED = [0, 1, 7, 2, 6, 3, 5, 4]
Y_PEERS = [y * 2 + core for core in range(2) for y in MIXED]


def swap(blocks, axis, peers=None):
    groups = None if peers is None else [peers]
    return lax.all_to_all(blocks, axis, split_axis=0, concat_axis=0, tiled=True, axis_index_groups=groups)


def split_rows(row):
    rows = jnp.concatenate([row[:, i * 128 : (i + 1) * 128] for i in range(4)], axis=0)
    high = rows.astype(bf16).astype(f32)
    low = rows - high
    return jnp.concatenate([high, low, jnp.zeros((8, 128), f32)], axis=0).astype(bf16)


def join_rows(rows):
    rows = rows.astype(f32)
    return rows[0:4] + rows[4:8]


def as_row(rows):
    return jnp.concatenate([rows[i : i + 1] for i in range(4)], axis=1)


def features_first(x_ref):
    x = x_ref[...].astype(f32).reshape(2, TP, 8, F)
    return jnp.concatenate([x[0][:, None], x[1][:, None]], axis=1).reshape(TOK, F).T


def key_kernel(key_ref, block_ref):
    for c in range(8):
        block_ref[c * 16 : (c + 1) * 16, :] = key_ref[:, c * 128 : (c + 1) * 128]


def first_kernel(flag_ref, x_ref, block_ref, send_ref, flags_ref):
    xt = features_first(x_ref)
    sums = split_rows(jnp.sum(xt * xt, axis=0, keepdims=True))
    for peer in range(NZ):
        send_ref[peer, 0:128, :] = block_ref[...]
        send_ref[peer, 128:136, :] = sums[0:8]
    flag = flag_ref[0]
    factor = jnp.where(flag == 0, 1.0, jnp.where(flag == 1, 0.5, 0.0)).astype(f32)
    keep = jnp.where(flag == 2, 0.0, 1.0).astype(f32)
    flags_ref[...] = jnp.concatenate([jnp.full((4, 128), factor), jnp.full((4, 128), keep)], axis=0)


def middle_kernel(got_ref, send_ref):
    total = jnp.zeros((4, 128), f32)
    for z in range(NZ):
        total = total + join_rows(got_ref[z, 128:136, :])
    sums = split_rows(as_row(total))
    for peer in range(NX):
        for r, z in enumerate(RING):
            send_ref[peer, z * 128 : (z + 1) * 128, :] = got_ref[r, 0:128, :]
        send_ref[peer, 1024:1032, :] = sums[0:8]


def main_kernel(
    flags_ref, x_ref, got_ref, gain_ref, master_ref, gw_ref, plain_ref, slope_ref, send_ref, rows_ref, gx_ref
):
    for x in range(NX):
        for z in range(NZ):
            slot = z * NX + x
            for c in range(8):
                rows_ref[slot * 16 : (slot + 1) * 16, c * 128 : (c + 1) * 128] = got_ref[
                    x, z * 128 + c * 16 : z * 128 + (c + 1) * 16, :
                ]
    total = jnp.zeros((4, 128), f32)
    for x in range(NX):
        total = total + join_rows(got_ref[x, 1024:1032, :])
    inv = lax.rsqrt(as_row(total) * (1.0 / D) + 1e-05)
    col = jnp.broadcast_to(gain_ref[...], (8, F)).T[:, 0:1]
    xt = features_first(x_ref)
    gx = xt * col
    gx_ref[...] = (gx * inv).astype(bf16)
    slope_ref[...] = xt * (inv * inv * inv * (1.0 / D))
    factor = flags_ref[0:1, 0:1]
    square = jnp.zeros((1, 256), f32)
    for n in range(4):
        cols = slice(n * 256, (n + 1) * 256)
        part = factor * jnp.dot(gx_ref[...], rows_ref[:, cols], preferred_element_type=f32)
        gw_ref[:, cols] = part
        square = square + jnp.sum(part * part, axis=0, keepdims=True)
    own_sq = jnp.broadcast_to(jnp.sum(square, axis=1, keepdims=True), (1, 128))
    weight = master_ref[...].astype(bf16)
    parts = []
    for n in range(2):
        cols = slice(n * 256, (n + 1) * 256)
        gh = lax.dot_general(
            weight, rows_ref[cols, :], (((1,), (1,)), ((), ())), preferred_element_type=f32
        )
        plain_ref[:, cols] = inv[:, cols] * (col * gh)
        parts.append(jnp.sum(gx[:, cols] * gh, axis=0, keepdims=True))
    packed = jnp.concatenate(parts + [own_sq], axis=1)
    for peer in range(TP):
        send_ref[peer] = packed


def branch_kernel(plain_ref, slope_ref, got_ref, send_ref):
    packed = got_ref[0]
    for peer in range(1, TP):
        packed = packed + got_ref[peer]
    sent = (plain_ref[...] - slope_ref[...] * packed[:, 0:TOK]).astype(bf16)
    layer_sq = split_rows(jnp.concatenate([packed[:, TOK:]] * 4, axis=1))
    for j in range(SEC):
        for q in range(4):
            send_ref[j, q * 16 : (q + 1) * 16, :] = sent[j * 16 : (j + 1) * 16, q * 128 : (q + 1) * 128]
        send_ref[j, 64:72, :] = layer_sq[0:8]


def suffix_kernel(got_ref, flags_ref, back_ref, clip_ref):
    running = jnp.zeros((64, 128), f32)
    norm = jnp.zeros((4, 128), f32)
    for layer in range(SEC - 1, -1, -1):
        s = Y_PEERS.index(layer)
        running = running + got_ref[s, 0:64, :].astype(f32)
        back_ref[s] = running.astype(bf16)
        norm = norm + join_rows(got_ref[s, 64:72, :])
    clip = jnp.minimum(1.0, clip_norm / (jnp.sqrt(norm) + 1e-06))
    clip_ref[...] = jnp.concatenate([clip, flags_ref[4:8, :]], axis=0)


def last_kernel(back_ref, out_ref):
    rows = []
    for j in range(SEC):
        rows.append(jnp.concatenate([back_ref[j, q * 16 : (q + 1) * 16, :] for q in range(4)], axis=1))
    out = jnp.concatenate(rows, axis=0).astype(f32).T.reshape(TP, 2, 8, F)
    for m in range(2):
        out_ref[m] = out[:, m].reshape(256, F).astype(bf16)


def on_device(hidden, gain, key_grad, master, moment, second, overflow):
    block = call(key_kernel, sds((128, 128), bf16), 1, 4 * F * TOK * K, 4 * 1024 * 1024)(key_grad.reshape(16, K))
    send, flags = call(
        first_kernel, (sds((NZ, 136, 128), bf16), sds((8, 128))), 2, 3 * F * TOK, F * TOK * 2, (), 1
    )(overflow, hidden[0], block)
    got = swap(send, "z", RING)
    send = call(middle_kernel, sds((NX, 1032, 128), bf16), 1, 0, 1024 * 1024)(got)
    got = swap(send, "x")
    gw, plain, slope, send = call(
        main_kernel,
        (sds((F, K)), sds((F, TOK)), sds((F, TOK)), sds((TP, 1, TOK + 128))),
        5,
        4 * F * TOK * K,
        4 * 1024 * 1024,
        [pltpu.VMEM((TOK, K), bf16), pltpu.VMEM((F, TOK), bf16)],
    )(flags, hidden[0], got, gain, master[0])
    got = swap(send, ("z", "x"))
    send = call(branch_kernel, sds((SEC, 72, 128), bf16), 3, 3 * F * TOK, 1024 * 1024)(plain, slope, got)
    got = swap(send, ("y", "core"), Y_PEERS)
    back, clip = call(
        suffix_kernel, (sds((SEC, 64, 128), bf16), sds((8, 128))), 2, 4 * F * TOK, 1024 * 1024
    )(got, flags)
    back = swap(back, ("y", "core"), Y_PEERS)
    clipped = clip[0, 0] * gw
    moment_new = beta_one * moment[0] + (1.0 - beta_one) * clipped
    second_new = beta_two * second[0] + (1.0 - beta_two) * clipped * clipped
    bias_one = 1.0 - beta_one**step_count
    bias_two = 1.0 - beta_two**step_count
    update = moment_new / bias_one / (jnp.sqrt(second_new / bias_two) + 1e-08) + decay * master[0]
    grad_input = call(last_kernel, sds((2, 256, F), bf16), 1, F * TOK, 1024 * 1024)(back)
    return (grad_input[None], (clip[4, 0] * update)[None])


def solution(mesh):
    fine = Mesh(mesh.devices.reshape(8, 2, NZ, NX), ("y", "core", "z", "x"))
    sec, tp = ("y", "core"), ("z", "x")
    return jax.shard_map(
        on_device,
        mesh=fine,
        in_specs=(
            P(sec, None, None, tp),
            P(sec, tp),
            P(sec, None, tp, None),
            P(sec, tp, None),
            P(sec, tp, None),
            P(sec, tp, None),
            P(sec),
        ),
        out_specs=(P(sec, None, None, tp), P(sec, tp, None)),
        check_vma=False,
    )
```

```python
import jax
import jax.numpy as jnp
from jax import lax
from jax.experimental import pallas as pl
from jax.experimental.pallas import tpu as pltpu
from jax.sharding import Mesh, PartitionSpec as P

D = 8192
SEC, NZ, NX = 16, 8, 4
TP = NZ * NX
TOK = 512
F = 256
K = 1024
f32, bf16 = jnp.float32, jnp.bfloat16

beta_one = 0.9
beta_two = 0.999
decay = 0.1
clip_norm = 1.0
step_count = 10

VM = pl.BlockSpec(memory_space=pltpu.VMEM)
SM = pl.BlockSpec(memory_space=pltpu.SMEM)


def call(body, out_shape, n_in, flops=0, data=0, scratch=(), scalars=0):
    outs = (VM,) * len(out_shape) if isinstance(out_shape, tuple) else VM
    return pl.pallas_call(
        body,
        out_shape=out_shape,
        in_specs=[SM] * scalars + [VM] * n_in,
        out_specs=outs,
        scratch_shapes=list(scratch),
        compiler_params=pltpu.CompilerParams(vmem_limit_bytes=32 * 1024 * 1024),
        cost_estimate=pl.CostEstimate(flops=flops, bytes_accessed=data, transcendentals=0),
    )


def sds(shape, dtype=f32):
    return jax.ShapeDtypeStruct(shape, dtype)


MIXED = [0, 1, 7, 2, 6, 3, 5, 4]
Y_PEERS = [y * 2 + core for core in range(2) for y in MIXED]


def swap(blocks, axis, peers=None):
    groups = None if peers is None else [peers]
    return lax.all_to_all(blocks, axis, split_axis=0, concat_axis=0, tiled=True, axis_index_groups=groups)


def split_rows(row):
    rows = jnp.concatenate([row[:, i * 128 : (i + 1) * 128] for i in range(4)], axis=0)
    high = rows.astype(bf16).astype(f32)
    low = rows - high
    return jnp.concatenate([high, low, jnp.zeros((8, 128), f32)], axis=0).astype(bf16)


def join_rows(rows):
    rows = rows.astype(f32)
    return rows[0:4] + rows[4:8]


def as_row(rows):
    return jnp.concatenate([rows[i : i + 1] for i in range(4)], axis=1)


def features_first(x_ref):
    x = x_ref[...].astype(f32).reshape(2, TP, 8, F)
    return jnp.concatenate([x[0][:, None], x[1][:, None]], axis=1).reshape(TOK, F).T


def key_kernel(key_ref, block_ref):
    for c in range(8):
        block_ref[c * 16 : (c + 1) * 16, :] = key_ref[:, c * 128 : (c + 1) * 128]


def first_kernel(flag_ref, x_ref, block_ref, send_ref, flags_ref):
    xt = features_first(x_ref)
    sums = split_rows(jnp.sum(xt * xt, axis=0, keepdims=True))
    for peer in range(NZ):
        send_ref[peer, 0:128, :] = block_ref[...]
        send_ref[peer, 128:136, :] = sums[0:8]
    flag = flag_ref[0]
    factor = jnp.where(flag == 0, 1.0, jnp.where(flag == 1, 0.5, 0.0)).astype(f32)
    keep = jnp.where(flag == 2, 0.0, 1.0).astype(f32)
    flags_ref[...] = jnp.concatenate([jnp.full((4, 128), factor), jnp.full((4, 128), keep)], axis=0)


def middle_kernel(got_ref, send_ref):
    total = jnp.zeros((4, 128), f32)
    for z in range(NZ):
        total = total + join_rows(got_ref[z, 128:136, :])
    sums = split_rows(as_row(total))
    for peer in range(NX):
        for r, z in enumerate(MIXED):
            send_ref[peer, z * 128 : (z + 1) * 128, :] = got_ref[r, 0:128, :]
        send_ref[peer, 1024:1032, :] = sums[0:8]


def main_kernel(
    flags_ref, x_ref, got_ref, gain_ref, master_ref, gw_ref, plain_ref, slope_ref, send_ref, rows_ref, gx_ref
):
    for x in range(NX):
        for z in range(NZ):
            slot = z * NX + x
            for c in range(8):
                rows_ref[slot * 16 : (slot + 1) * 16, c * 128 : (c + 1) * 128] = got_ref[
                    x, z * 128 + c * 16 : z * 128 + (c + 1) * 16, :
                ]
    total = jnp.zeros((4, 128), f32)
    for x in range(NX):
        total = total + join_rows(got_ref[x, 1024:1032, :])
    inv = lax.rsqrt(as_row(total) * (1.0 / D) + 1e-05)
    col = jnp.broadcast_to(gain_ref[...], (8, F)).T[:, 0:1]
    xt = features_first(x_ref)
    gx = xt * col
    gx_ref[...] = (gx * inv).astype(bf16)
    slope_ref[...] = xt * (inv * inv * inv * (1.0 / D))
    factor = flags_ref[0:1, 0:1]
    square = jnp.zeros((1, 256), f32)
    for n in range(4):
        cols = slice(n * 256, (n + 1) * 256)
        part = factor * jnp.dot(gx_ref[...], rows_ref[:, cols], preferred_element_type=f32)
        gw_ref[:, cols] = part
        square = square + jnp.sum(part * part, axis=0, keepdims=True)
    own_sq = jnp.broadcast_to(jnp.sum(square, axis=1, keepdims=True), (1, 128))
    weight = master_ref[...].astype(bf16)
    parts = []
    for n in range(2):
        cols = slice(n * 256, (n + 1) * 256)
        gh = lax.dot_general(
            weight, rows_ref[cols, :], (((1,), (1,)), ((), ())), preferred_element_type=f32
        )
        plain_ref[:, cols] = inv[:, cols] * (col * gh)
        parts.append(jnp.sum(gx[:, cols] * gh, axis=0, keepdims=True))
    packed = jnp.concatenate(parts + [own_sq], axis=1)
    for peer in range(TP):
        send_ref[peer] = packed


def branch_kernel(plain_ref, slope_ref, got_ref, send_ref):
    packed = got_ref[0]
    for peer in range(1, TP):
        packed = packed + got_ref[peer]
    sent = (plain_ref[...] - slope_ref[...] * packed[:, 0:TOK]).astype(bf16)
    layer_sq = split_rows(jnp.concatenate([packed[:, TOK:]] * 4, axis=1))
    for j in range(SEC):
        for q in range(4):
            send_ref[j, q * 16 : (q + 1) * 16, :] = sent[j * 16 : (j + 1) * 16, q * 128 : (q + 1) * 128]
        send_ref[j, 64:72, :] = layer_sq[0:8]


def suffix_kernel(got_ref, flags_ref, back_ref, clip_ref):
    running = jnp.zeros((64, 128), f32)
    norm = jnp.zeros((4, 128), f32)
    for layer in range(SEC - 1, -1, -1):
        s = Y_PEERS.index(layer)
        running = running + got_ref[s, 0:64, :].astype(f32)
        back_ref[s] = running.astype(bf16)
        norm = norm + join_rows(got_ref[s, 64:72, :])
    clip = jnp.minimum(1.0, clip_norm / (jnp.sqrt(norm) + 1e-06))
    clip_ref[...] = jnp.concatenate([clip, flags_ref[4:8, :]], axis=0)


def last_kernel(back_ref, out_ref):
    rows = []
    for j in range(SEC):
        rows.append(jnp.concatenate([back_ref[j, q * 16 : (q + 1) * 16, :] for q in range(4)], axis=1))
    out = jnp.concatenate(rows, axis=0).astype(f32).T.reshape(TP, 2, 8, F)
    for m in range(2):
        out_ref[m] = out[:, m].reshape(256, F).astype(bf16)


def on_device(hidden, gain, key_grad, master, moment, second, overflow):
    block = call(key_kernel, sds((128, 128), bf16), 1, 4 * F * TOK * K, 4 * 1024 * 1024)(key_grad.reshape(16, K))
    send, flags = call(
        first_kernel, (sds((NZ, 136, 128), bf16), sds((8, 128))), 2, 3 * F * TOK, F * TOK * 2, (), 1
    )(overflow, hidden[0], block)
    got = swap(send, "z", MIXED)
    send = call(middle_kernel, sds((NX, 1032, 128), bf16), 1, 0, 1024 * 1024)(got)
    got = swap(send, "x")
    gw, plain, slope, send = call(
        main_kernel,
        (sds((F, K)), sds((F, TOK)), sds((F, TOK)), sds((TP, 1, TOK + 128))),
        5,
        4 * F * TOK * K,
        4 * 1024 * 1024,
        [pltpu.VMEM((TOK, K), bf16), pltpu.VMEM((F, TOK), bf16)],
    )(flags, hidden[0], got, gain, master[0])
    got = swap(send, ("z", "x"))
    send = call(branch_kernel, sds((SEC, 72, 128), bf16), 3, 3 * F * TOK, 1024 * 1024)(plain, slope, got)
    got = swap(send, ("y", "core"), Y_PEERS)
    back, clip = call(
        suffix_kernel, (sds((SEC, 64, 128), bf16), sds((8, 128))), 2, 4 * F * TOK, 1024 * 1024
    )(got, flags)
    back = swap(back, ("y", "core"), Y_PEERS)
    clipped = clip[0, 0] * gw
    moment_new = beta_one * moment[0] + (1.0 - beta_one) * clipped
    second_new = beta_two * second[0] + (1.0 - beta_two) * clipped * clipped
    bias_one = 1.0 - beta_one**step_count
    bias_two = 1.0 - beta_two**step_count
    update = moment_new / bias_one / (jnp.sqrt(second_new / bias_two) + 1e-08) + decay * master[0]
    grad_input = call(last_kernel, sds((2, 256, F), bf16), 1, F * TOK, 1024 * 1024)(back)
    return (grad_input[None], (clip[4, 0] * update)[None])


def solution(mesh):
    fine = Mesh(mesh.devices.reshape(8, 2, NZ, NX), ("y", "core", "z", "x"))
    sec, tp = ("y", "core"), ("z", "x")
    return jax.shard_map(
        on_device,
        mesh=fine,
        in_specs=(
            P(sec, None, None, tp),
            P(sec, tp),
            P(sec, None, tp, None),
            P(sec, tp, None),
            P(sec, tp, None),
            P(sec, tp, None),
            P(sec),
        ),
        out_specs=(P(sec, None, None, tp), P(sec, tp, None)),
        check_vma=False,
    )
```

```python
import jax
import jax.numpy as jnp
from jax import lax
from jax.experimental import pallas as pl
from jax.experimental.pallas import tpu as pltpu
from jax.sharding import Mesh, PartitionSpec as P

D = 8192
SEC, NZ, NX = 16, 8, 4
TP = NZ * NX
TOK = 512
F = 256
K = 1024
f32, bf16 = jnp.float32, jnp.bfloat16

beta_one = 0.9
beta_two = 0.999
decay = 0.1
clip_norm = 1.0
step_count = 10

VM = pl.BlockSpec(memory_space=pltpu.VMEM)
SM = pl.BlockSpec(memory_space=pltpu.SMEM)


def call(body, out_shape, n_in, flops=0, data=0, scratch=(), scalars=0):
    outs = (VM,) * len(out_shape) if isinstance(out_shape, tuple) else VM
    return pl.pallas_call(
        body,
        out_shape=out_shape,
        in_specs=[SM] * scalars + [VM] * n_in,
        out_specs=outs,
        scratch_shapes=list(scratch),
        compiler_params=pltpu.CompilerParams(vmem_limit_bytes=32 * 1024 * 1024),
        cost_estimate=pl.CostEstimate(flops=flops, bytes_accessed=data, transcendentals=0),
    )


def sds(shape, dtype=f32):
    return jax.ShapeDtypeStruct(shape, dtype)


MIXED = [0, 1, 7, 2, 6, 3, 5, 4]
Y_PEERS = [y * 2 + core for core in range(2) for y in MIXED]


def swap(blocks, axis, peers=None):
    groups = None if peers is None else [peers]
    return lax.all_to_all(blocks, axis, split_axis=0, concat_axis=0, tiled=True, axis_index_groups=groups)


def split_rows(row):
    rows = jnp.concatenate([row[:, i * 128 : (i + 1) * 128] for i in range(4)], axis=0)
    high = rows.astype(bf16).astype(f32)
    low = rows - high
    return jnp.concatenate([high, low, jnp.zeros((8, 128), f32)], axis=0).astype(bf16)


def join_rows(rows):
    rows = rows.astype(f32)
    return rows[0:4] + rows[4:8]


def as_row(rows):
    return jnp.concatenate([rows[i : i + 1] for i in range(4)], axis=1)


def features_first(x_ref):
    x = x_ref[...].astype(f32).reshape(2, TP, 8, F)
    return jnp.concatenate([x[0][:, None], x[1][:, None]], axis=1).reshape(TOK, F).T


def key_kernel(key_ref, block_ref):
    for c in range(8):
        block_ref[c * 16 : (c + 1) * 16, :] = key_ref[:, c * 128 : (c + 1) * 128]


def first_kernel(flag_ref, x_ref, block_ref, send_ref, flags_ref):
    xt = features_first(x_ref)
    sums = split_rows(jnp.sum(xt * xt, axis=0, keepdims=True))
    for peer in range(NZ):
        send_ref[peer, 0:128, :] = block_ref[...]
        send_ref[peer, 128:144, :] = sums
    flag = flag_ref[0]
    factor = jnp.where(flag == 0, 1.0, jnp.where(flag == 1, 0.5, 0.0)).astype(f32)
    keep = jnp.where(flag == 2, 0.0, 1.0).astype(f32)
    flags_ref[...] = jnp.concatenate([jnp.full((4, 128), factor), jnp.full((4, 128), keep)], axis=0)


def middle_kernel(got_ref, send_ref):
    total = jnp.zeros((4, 128), f32)
    for z in range(NZ):
        total = total + join_rows(got_ref[z, 128:144, :])
    sums = split_rows(as_row(total))
    for peer in range(NX):
        for r, z in enumerate(MIXED):
            send_ref[peer, z * 128 : (z + 1) * 128, :] = got_ref[r, 0:128, :]
        send_ref[peer, 1024:1040, :] = sums


def main_kernel(
    flags_ref, x_ref, got_ref, gain_ref, master_ref, gw_ref, plain_ref, slope_ref, send_ref, rows_ref, gx_ref
):
    for x in range(NX):
        for z in range(NZ):
            slot = z * NX + x
            for c in range(8):
                rows_ref[slot * 16 : (slot + 1) * 16, c * 128 : (c + 1) * 128] = got_ref[
                    x, z * 128 + c * 16 : z * 128 + (c + 1) * 16, :
                ]
    total = jnp.zeros((4, 128), f32)
    for x in range(NX):
        total = total + join_rows(got_ref[x, 1024:1040, :])
    inv = lax.rsqrt(as_row(total) * (1.0 / D) + 1e-05)
    col = jnp.broadcast_to(gain_ref[...], (8, F)).T[:, 0:1]
    xt = features_first(x_ref)
    gx = xt * col
    gx_ref[...] = (gx * inv).astype(bf16)
    slope_ref[...] = xt * (inv * inv * inv * (1.0 / D))
    factor = flags_ref[0:1, 0:1]
    square = jnp.zeros((1, 256), f32)
    for n in range(4):
        cols = slice(n * 256, (n + 1) * 256)
        part = factor * jnp.dot(gx_ref[...], rows_ref[:, cols], preferred_element_type=f32)
        gw_ref[:, cols] = part
        square = square + jnp.sum(part * part, axis=0, keepdims=True)
    own_sq = jnp.broadcast_to(jnp.sum(square, axis=1, keepdims=True), (1, 128))
    weight = master_ref[...].astype(bf16)
    parts = []
    for n in range(2):
        cols = slice(n * 256, (n + 1) * 256)
        gh = lax.dot_general(
            weight, rows_ref[cols, :], (((1,), (1,)), ((), ())), preferred_element_type=f32
        )
        plain_ref[:, cols] = inv[:, cols] * (col * gh)
        parts.append(jnp.sum(gx[:, cols] * gh, axis=0, keepdims=True))
    packed = jnp.concatenate(parts + [own_sq], axis=1)
    for peer in range(TP):
        send_ref[peer] = packed


def branch_kernel(plain_ref, slope_ref, got_ref, send_ref):
    packed = got_ref[0]
    for peer in range(1, TP):
        packed = packed + got_ref[peer]
    sent = (plain_ref[...] - slope_ref[...] * packed[:, 0:TOK]).astype(bf16)
    layer_sq = split_rows(jnp.concatenate([packed[:, TOK:]] * 4, axis=1))
    for j in range(SEC):
        for q in range(4):
            send_ref[j, q * 16 : (q + 1) * 16, :] = sent[j * 16 : (j + 1) * 16, q * 128 : (q + 1) * 128]
        send_ref[j, 64:80, :] = layer_sq


def suffix_kernel(got_ref, flags_ref, back_ref, clip_ref):
    running = jnp.zeros((64, 128), f32)
    norm = jnp.zeros((4, 128), f32)
    for layer in range(SEC - 1, -1, -1):
        s = Y_PEERS.index(layer)
        running = running + got_ref[s, 0:64, :].astype(f32)
        back_ref[s] = running.astype(bf16)
        norm = norm + join_rows(got_ref[s, 64:80, :])
    clip = jnp.minimum(1.0, clip_norm / (jnp.sqrt(norm) + 1e-06))
    clip_ref[...] = jnp.concatenate([clip, flags_ref[4:8, :]], axis=0)


def last_kernel(back_ref, out_ref):
    rows = []
    for j in range(SEC):
        rows.append(jnp.concatenate([back_ref[j, q * 16 : (q + 1) * 16, :] for q in range(4)], axis=1))
    out = jnp.concatenate(rows, axis=0).astype(f32).T.reshape(TP, 2, 8, F)
    for m in range(2):
        out_ref[m] = out[:, m].reshape(256, F).astype(bf16)


def on_device(hidden, gain, key_grad, master, moment, second, overflow):
    block = call(key_kernel, sds((128, 128), bf16), 1, 4 * F * TOK * K, 4 * 1024 * 1024)(key_grad.reshape(16, K))
    send, flags = call(
        first_kernel, (sds((NZ, 144, 128), bf16), sds((8, 128))), 2, 3 * F * TOK, F * TOK * 2, (), 1
    )(overflow, hidden[0], block)
    got = swap(send, "z", MIXED)
    send = call(middle_kernel, sds((NX, 1040, 128), bf16), 1, 0, 1024 * 1024)(got)
    got = swap(send, "x")
    gw, plain, slope, send = call(
        main_kernel,
        (sds((F, K)), sds((F, TOK)), sds((F, TOK)), sds((TP, 1, TOK + 128))),
        5,
        4 * F * TOK * K,
        4 * 1024 * 1024,
        [pltpu.VMEM((TOK, K), bf16), pltpu.VMEM((F, TOK), bf16)],
    )(flags, hidden[0], got, gain, master[0])
    got = swap(send, ("z", "x"))
    send = call(branch_kernel, sds((SEC, 80, 128), bf16), 3, 3 * F * TOK, 1024 * 1024)(plain, slope, got)
    got = swap(send, ("y", "core"), Y_PEERS)
    back, clip = call(
        suffix_kernel, (sds((SEC, 64, 128), bf16), sds((8, 128))), 2, 4 * F * TOK, 1024 * 1024
    )(got, flags)
    back = swap(back, ("y", "core"), Y_PEERS)
    clipped = clip[0, 0] * gw
    moment_new = beta_one * moment[0] + (1.0 - beta_one) * clipped
    second_new = beta_two * second[0] + (1.0 - beta_two) * clipped * clipped
    bias_one = 1.0 - beta_one**step_count
    bias_two = 1.0 - beta_two**step_count
    update = moment_new / bias_one / (jnp.sqrt(second_new / bias_two) + 1e-08) + decay * master[0]
    grad_input = call(last_kernel, sds((2, 256, F), bf16), 1, F * TOK, 1024 * 1024)(back)
    return (grad_input[None], (clip[4, 0] * update)[None])


def solution(mesh):
    fine = Mesh(mesh.devices.reshape(8, 2, NZ, NX), ("y", "core", "z", "x"))
    sec, tp = ("y", "core"), ("z", "x")
    return jax.shard_map(
        on_device,
        mesh=fine,
        in_specs=(
            P(sec, None, None, tp),
            P(sec, tp),
            P(sec, None, tp, None),
            P(sec, tp, None),
            P(sec, tp, None),
            P(sec, tp, None),
            P(sec),
        ),
        out_specs=(P(sec, None, None, tp), P(sec, tp, None)),
        check_vma=False,
    )
```
